512 devices in a mesh: rows: 32 (over x, y), depth: 16 (over z, core).
Axes of the slice: x: 4, y: 8, z: 8, core: 2. Of those that a mesh axis runs over, the one named last changes fastest.
Arguments:
- left_factors: bfloat16 [32, 32, 2048, 128], P('rows', 'depth'), may hold values from -0.125 to 0.125
- right_factors: bfloat16 [32, 32, 2048, 128], P('rows', 'depth'), may hold values from -0.125 to 0.125
- probe_matrix: bfloat16 [2048, 128], replicated, may hold values from -6 to 6
- tile_list: int32 [32, 4], replicated, may hold values from 0 to 31, all different within a row
Outputs:
- basis: float32 [32, 4, 2048, 128], P('rows', None, 'depth')
- chol_factor: float32 [32, 4, 128, 128], P('rows')
The draws below stay inside these ranges and needn't reach their ends.
Inputs may be any that keep to these rules, and one draw needn't show every extreme that they name: `tile_list`: each row holds 4 different tile rows, and every tile row is named by some row.
All inputs are finite; a program needn't handle non-finite values.
Results may differ from the reference program's by a relative error of at most 0.0058.
Values may be sent and summed in bfloat16 or wider, within the bound.
A program may use at most 64 MiB of HBM per device.

```python
import math
import jax
import jax.numpy as jnp
from jax import lax

TILE = 2048
RANK = 128
TLIST = 4
NTILE = 32
PANELS = 32


def shard_levels(own_key, dims, split, smallest, largest):
    gain, own = 1.0, jax.random.fold_in(own_key, 6)
    for axis_at, parts in split:
        heights = jnp.exp(jax.random.uniform(jax.random.fold_in(own, axis_at), (parts,), jnp.float32, smallest / len(split), largest / len(split)))
        gain = gain * jnp.repeat(heights, dims[axis_at] // parts).reshape([-1 if axis == axis_at else 1 for axis in range(len(dims))])
    return gain


def distinct(own_key, rows, number_of, top, lift):
    ranking = jax.random.permutation(jax.random.fold_in(own_key, 1), number_of)
    favour = ranking
    for power in range(3):
        favour = favour * favour // number_of
    favour = favour * lift // number_of
    lots = jax.random.randint(jax.random.fold_in(own_key, 2), (rows, number_of), 0, 4096) + favour
    holders = jax.random.permutation(jax.random.fold_in(own_key, 3), rows)[jnp.arange(number_of) % rows]
    lots = jnp.where(jnp.arange(rows)[:, None] == holders[None, :], 1 << 14, lots)
    merit = lots * number_of + jnp.arange(number_of)
    return lax.top_k(merit.astype(jnp.int32), top)[1].astype(jnp.int32)


def scatter_about(stream_key, extent, deviation, bound, split=(), kind=jnp.bfloat16):
    result = jax.random.normal(stream_key, extent, jnp.float32) * deviation
    if len(split) > 0:
        result = shard_levels(stream_key, extent, split, -0.22, 0.18) * result
    return jnp.clip(result, min=-bound, max=bound).astype(kind)


def setup_inputs(seed: int = 0) -> dict:
    keys = jax.random.split(jax.random.key(seed), 5)
    return {
        "left_factors": scatter_about(keys[0], (NTILE, PANELS, TILE, RANK), TILE ** -0.5, 0.125, ((0, 32), (1, 16))),
        "right_factors": scatter_about(keys[1], (NTILE, PANELS, TILE, RANK), TILE ** -0.5, 0.125, ((0, 32), (1, 16))),
        "probe_matrix": scatter_about(keys[2], (TILE, RANK), 1.0, 6.0),
        "tile_list": distinct(keys[3], NTILE, NTILE, TLIST, 2048),
    }


def reference(left_factors, right_factors, probe_matrix, tile_list):
    probe32 = probe_matrix.astype(jnp.float32)

    def sketch_one(pair):
        left_row, right_row = pair
        image = jnp.einsum('pbk,bl->pkl', left_row.astype(jnp.float32), probe32).astype(jnp.bfloat16)
        return jnp.einsum('pbk,pkl->pbl', right_row.astype(jnp.float32), image.astype(jnp.float32)).astype(jnp.bfloat16)
    sketch_rows = lax.map(sketch_one, (left_factors, right_factors))
    scale = math.sqrt(float(TILE))

    def update_row(triple):
        left_row, right_row, listed = triple
        picked = jnp.take(sketch_rows, listed.astype(jnp.int32), axis=0)
        coupling = jnp.einsum('pbk,tpbl->tpkl', right_row.astype(jnp.float32), picked.astype(jnp.float32)).astype(jnp.bfloat16)
        sketch = jnp.einsum('pbk,tpkl->tbl', left_row.astype(jnp.float32), coupling.astype(jnp.float32))
        gram = jnp.einsum('tbk,tbl->tkl', sketch, sketch, precision=lax.Precision.HIGHEST)
        lower = jnp.linalg.cholesky(gram)
        solved = jax.scipy.linalg.solve_triangular(lower, jnp.transpose(sketch, (0, 2, 1)), lower=True)
        return (jnp.transpose(solved, (0, 2, 1)) * scale, lower / scale)
    basis, chol_factor = lax.map(update_row, (left_factors, right_factors, tile_list))
    return (basis, chol_factor)
```

```python
import functools
import math

import jax
import jax.numpy as jnp
from jax import lax
from jax.experimental import pallas as pl
from jax.experimental.pallas import tpu as pltpu
from jax.sharding import PartitionSpec as P

MESH = pl.DeviceIdType.MESH
F32 = jnp.float32
BF16 = jnp.bfloat16
XS = 4
CORES = 2
HIGHEST = lax.Precision.HIGHEST


def spiral(count):
    order = [0]
    for step in range(1, count // 2 + 1):
        order.append(step)
        if count - step != step:
            order.append(count - step)
    return order[:count]


def spiral_at(s, count):
    half = lax.div(s + 1, 2)
    return jnp.where(lax.rem(s, 2) == 1, half, lax.rem(count - half, count))


def rcopy(src, dst, send_sem, recv_sem, device):
    return pltpu.make_async_remote_copy(
        src_ref=src, dst_ref=dst, send_sem=send_sem, recv_sem=recv_sem,
        device_id=device, device_id_type=MESH)


def tdot(a, b, precision=None):
    return lax.dot_general(a, b, (((0,), (0,)), ((), ())), precision=precision,
                           preferred_element_type=F32)


def coupling_kernel(xs, ys, tile_ref, u_ref, v_ref, om_ref, out_ref,
                    vb0, vb1, ma0, ma1, sa0, sa1, stage, rbuf,
                    own_sem, v_send, v_recv, m_send, m_recv,
                    s_send, f_send, s_recv, r_send, r_recv):
    vb, ma, sa = (vb0, vb1), (ma0, ma1), (sa0, sa1)
    panels = 2
    me = lax.axis_index("rows")
    x, y = lax.div(me, ys), lax.rem(me, ys)
    rows = vb0.shape[1]
    rank = ma0.shape[1]
    listed = tile_ref.shape[1]

    def at(xx, yy):
        return {"rows": lax.rem(xx, xs) * ys + lax.rem(yy, ys)}

    barrier = pltpu.get_barrier_semaphore()
    for dy in range(1, ys):
        pl.semaphore_signal(barrier, inc=1, device_id=at(x, y + dy), device_id_type=MESH)
    for dx in (1, xs - 1):
        pl.semaphore_signal(barrier, inc=1, device_id=at(x + dx, y), device_id_type=MESH)

    own = []
    for p in range(panels):
        own.append(pltpu.make_async_copy(
            v_ref.at[p, pl.ds(pl.multiple_of(y * rows, rows), rows), :],
            vb[p].at[y], own_sem.at[p]))
        own[p].start()
    pl.semaphore_wait(barrier, ys + 1)

    def send_v(p):
        def body(s, carry):
            yd = lax.rem(y + spiral_at(s, ys), ys)
            rcopy(v_ref.at[p, pl.ds(pl.multiple_of(yd * rows, rows), rows), :],
                  vb[p].at[y], v_send.at[p, s], v_recv.at[p, y], at(x, yd)).start()
            return carry
        lax.fori_loop(1, ys, body, 0)

    def send_m(p):
        ma[p][y] = tdot(u_ref[p], om_ref[...]).astype(BF16)

        def body(s, carry):
            yd = lax.rem(y + spiral_at(s, ys), ys)
            rcopy(ma[p].at[y], ma[p].at[y], m_send.at[p, s], m_recv.at[p, y],
                  at(x, yd)).start()
            return carry
        lax.fori_loop(1, ys, body, 0)

    def wait_in(ref, sem):
        rcopy(ref, ref, sem, sem, at(x, y)).wait_recv()

    def wait_out(ref, sem):
        rcopy(ref, ref, sem, sem, at(x, y)).wait_send()

    def sketch_block(p, yd):
        block = x * ys + yd
        sa[p][block] = jnp.dot(vb[p][yd], ma[p][yd], preferred_element_type=F32).astype(BF16)
        for side, dx in enumerate((1, xs - 1)):
            rcopy(sa[p].at[block], sa[p].at[block], s_send.at[p, side, yd],
                  s_recv.at[p, block], at(x + dx, y)).start()

    def forward(p, yd):
        come, go = ((xs - 1, 1), (1, xs - 1))[p]
        block = lax.rem(x + come, xs) * ys + yd
        wait_in(sa[p].at[block], s_recv.at[p, block])
        rcopy(sa[p].at[block], sa[p].at[block], f_send.at[p, yd],
              s_recv.at[p, block], at(x + go, y)).start()

    def sketch_panel(p):
        own[p].wait()
        sketch_block(p, y)

        def body(s, carry):
            yd = lax.rem(y + spiral_at(s, ys), ys)
            wait_in(vb[p].at[yd], v_recv.at[p, yd])
            wait_in(ma[p].at[yd], m_recv.at[p, yd])
            sketch_block(p, yd)
            forward(p, lax.rem(y + spiral_at(s - 1, ys), ys))
            return carry
        lax.fori_loop(1, ys, body, 0)
        forward(p, lax.rem(y + spiral_at(ys - 1, ys), ys))

    def rest_in(p):
        def body(yd, carry):
            for dx in ((1, 2), (2, xs - 1))[p]:
                block = lax.rem(x + dx, xs) * ys + yd
                wait_in(sa[p].at[block], s_recv.at[p, block])
            return carry
        lax.fori_loop(0, ys, body, 0)

    def part(p, yd):
        row = x * ys + yd
        picked = jnp.concatenate([sa[p][tile_ref[row, t]] for t in range(listed)], axis=1)
        return tdot(vb[p][yd], picked)

    chain = ((ys // 2, ys - 1 - ys // 2), (ys - 1 - ys // 2, ys // 2))

    def ring_step(p, s):
        for side in range(2):
            length = chain[p][side]
            if s >= length:
                continue
            away = length - s
            yd = lax.rem(y + (away if side == 0 else ys - away), ys)
            term = part(p, yd)
            if s > 0:
                wait_in(rbuf.at[p, side, s - 1], r_recv.at[p, side, s - 1])
                term = term + rbuf[p, side, s - 1].astype(F32)
            stage[p, side, s] = term.astype(BF16)
            rcopy(stage.at[p, side, s], rbuf.at[p, side, s], r_send.at[p, side, s],
                  r_recv.at[p, side, s], at(x, y + (1 if side == 0 else ys - 1))).start()

    def ring_end(p):
        term = part(p, y)
        for side in range(2):
            last = chain[p][side] - 1
            wait_in(rbuf.at[p, side, last], r_recv.at[p, side, last])
            term = term + rbuf[p, side, last].astype(F32)
        out_ref[p * rank:(p + 1) * rank, :] = term.astype(BF16)

    send_v(0)
    send_m(0)
    send_m(1)
    send_v(1)
    sketch_panel(0)
    sketch_panel(1)
    for p in range(panels):
        rest_in(p)
        for s in range(ys // 2):
            ring_step(p, s)
        ring_end(p)

    for p in range(panels):
        def drain(s, carry):
            wait_out(vb[p].at[y], v_send.at[p, s])
            wait_out(ma[p].at[y], m_send.at[p, s])
            return carry
        lax.fori_loop(1, ys, drain, 0)

        def drain_s(yd, carry):
            for side in range(2):
                wait_out(sa[p].at[yd], s_send.at[p, side, yd])
            wait_out(sa[p].at[yd], f_send.at[p, yd])
            return carry
        lax.fori_loop(0, ys, drain_s, 0)
        for side in range(2):
            for s in range(chain[p][side]):
                wait_out(stage.at[p, side, s], r_send.at[p, side, s])


def sum_kernel(zs, u_ref, c_ref, rows_ref, gram_ref,
               xsend, xrecv, held, stage, rbuf, gpart, gx, ghalf, gr, gsum, gall, gout,
               x_send, x_recv, r_send, r_recv, g_send, g_recv,
               a_send, a_recv, b_send, b_recv, e_send, e_recv):
    me = lax.axis_index("depth")
    z, c = lax.div(me, CORES), lax.rem(me, CORES)
    rows, width = rows_ref.shape
    half = width // 2
    rank = gram_ref.shape[1]
    tiles = width // rank
    panels = u_ref.shape[0]

    def at(zz, cc):
        return {"depth": lax.rem(zz, zs) * CORES + cc}

    def wait_in(ref, sem):
        rcopy(ref, ref, sem, sem, at(z, c)).wait_recv()

    def wait_out(ref, sem):
        rcopy(ref, ref, sem, sem, at(z, c)).wait_send()

    barrier = pltpu.get_barrier_semaphore()
    for dz in range(1, zs):
        pl.semaphore_signal(barrier, inc=1, device_id=at(z + dz, c), device_id_type=MESH)
    pl.semaphore_signal(barrier, inc=1, device_id=at(z, 1 - c), device_id_type=MESH)

    def block(zd, cd):
        start = pl.multiple_of((zd * CORES + cd) * rows, rows)
        left = jnp.concatenate([u_ref[p, pl.ds(start, rows), :] for p in range(panels)], axis=1)
        return jnp.dot(left, c_ref[...], preferred_element_type=F32)

    chain = ((zs // 2, zs - 1 - zs // 2), (zs - 1 - zs // 2, zs // 2))
    far_first = [zs // 2]
    for away in range(zs // 2 - 1, 0, -1):
        far_first += [away, zs - away]
    far_first.append(0)

    pl.semaphore_wait(barrier, zs)
    for away in far_first:
        zd = lax.rem(z + away, zs)
        xsend[zd] = block(zd, 1 - c)
        rcopy(xsend.at[zd], xrecv.at[zd], x_send.at[zd], x_recv.at[zd], at(z, 1 - c)).start()
    for away in far_first:
        zd = lax.rem(z + away, zs)
        mine = block(zd, c)
        wait_in(xrecv.at[zd], x_recv.at[zd])
        held[zd] = mine + xrecv[zd]

    for s in range(zs // 2):
        for h in range(2):
            for side in range(2):
                length = chain[h][side]
                if s >= length:
                    continue
                away = length - s
                zd = lax.rem(z + (away if side == 0 else zs - away), zs)
                term = held[zd, :, h * half:(h + 1) * half]
                if s > 0:
                    wait_in(rbuf.at[h, side, s - 1], r_recv.at[h, side, s - 1])
                    term = term + rbuf[h, side, s - 1].astype(F32)
                stage[h, side, s] = term.astype(BF16)
                rcopy(stage.at[h, side, s], rbuf.at[h, side, s], r_send.at[h, side, s],
                      r_recv.at[h, side, s], at(z + (1 if side == 0 else zs - 1), c)).start()
    for h in range(2):
        term = held[z, :, h * half:(h + 1) * half]
        for side in range(2):
            last = chain[h][side] - 1
            wait_in(rbuf.at[h, side, last], r_recv.at[h, side, last])
            term = term + rbuf[h, side, last].astype(F32)
        rows_ref[:, h * half:(h + 1) * half] = term

    for t in range(tiles):
        own = rows_ref[:, t * rank:(t + 1) * rank]
        gpart[t * rank:(t + 1) * rank, :] = tdot(own, own, HIGHEST)
    size = tiles * rank // CORES
    piece = size // zs
    theirs = pl.ds(pl.multiple_of((1 - c) * size, size), size)
    mine = pl.ds(pl.multiple_of(c * size, size), size)
    rcopy(gpart.at[theirs, :], gx, g_send, g_recv, at(z, 1 - c)).start()
    wait_in(gx, g_recv)
    ghalf[...] = gpart[mine, :] + gx[...]

    def piece_of(zd):
        return pl.ds(pl.multiple_of(zd * piece, piece), piece)

    for dz in range(1, zs):
        zd = lax.rem(z + dz, zs)
        rcopy(ghalf.at[piece_of(zd), :], gr.at[z], a_send.at[zd], a_recv.at[z], at(zd, c)).start()
    gr[z] = ghalf[piece_of(z), :]
    for dz in range(1, zs):
        zd = lax.rem(z + dz, zs)
        wait_in(gr.at[zd], a_recv.at[zd])
    total = gr[0]
    for k in range(1, zs):
        total = total + gr[k]
    gall[piece_of(z), :] = total
    for dz in range(1, zs):
        zd = lax.rem(z + dz, zs)
        rcopy(gall.at[piece_of(z), :], gall.at[piece_of(z), :], b_send.at[zd], b_recv.at[z],
              at(zd, c)).start()
    for dz in range(1, zs):
        zd = lax.rem(z + dz, zs)
        wait_in(gall.at[piece_of(zd), :], b_recv.at[zd])
    rcopy(gall, gout, e_send, e_recv, at(z, 1 - c)).start()
    gram_ref[mine, :] = gall[...]
    wait_in(gout, e_recv)
    gram_ref[theirs, :] = gout[...]

    for zd in range(zs):
        wait_out(xsend.at[zd], x_send.at[zd])
    for h in range(2):
        for side in range(2):
            for s in range(chain[h][side]):
                wait_out(stage.at[h, side, s], r_send.at[h, side, s])
    wait_out(gx, g_send)
    for dz in range(1, zs):
        zd = lax.rem(z + dz, zs)
        wait_out(gr.at[zd], a_send.at[zd])
        wait_out(gr.at[zd], b_send.at[zd])
    wait_out(gall, e_send)


def factor_kernel(scale, rows_ref, gram_ref, basis_ref, chol_ref):
    rank = gram_ref.shape[1]
    tiles = gram_ref.shape[0] // rank
    size = 128 // tiles
    lane = lax.broadcasted_iota(jnp.int32, (size, 128), 1)
    sub = lax.broadcasted_iota(jnp.int32, (size, 128), 0)
    first = (lane // size) * size
    unit = (lane - first == sub).astype(F32)

    def dott(a, b):
        return lax.dot_general(a, b, (((1,), (1,)), ((), ())), precision=HIGHEST,
                               preferred_element_type=F32)

    def dot(a, b):
        return jnp.dot(a, b, precision=HIGHEST, preferred_element_type=F32)

    trail = [gram_ref[t * rank:(t + 1) * rank, :] for t in range(tiles)]
    eye = (lax.broadcasted_iota(jnp.int32, (rank, rank), 0)
           == lax.broadcasted_iota(jnp.int32, (rank, rank), 1)).astype(F32)
    rest_inv = [eye] * tiles
    done = [[] for _ in range(tiles)]
    for b in range(rank // size):
        packed = jnp.concatenate([trail[t][:size, :size] for t in range(tiles)], axis=1)
        inv = unit
        pivots = jnp.ones((size, 128), F32)
        for k in range(size):
            column = jnp.take_along_axis(packed, first + k, axis=1)
            pivot = column[k:k + 1, :]
            times = jnp.where(sub > k, column / pivot, 0.0)
            pivots = jnp.where(sub == k, pivot, pivots)
            packed = packed - times * packed[k:k + 1, :]
            inv = inv - times * inv[k:k + 1, :]
        inv = inv * lax.rsqrt(pivots)
        for t in range(tiles):
            small = inv[:, t * size:(t + 1) * size]
            head = dot(small, rest_inv[t][:size, :])
            done[t].append(head)
            if (b + 1) * size < rank:
                below = dott(trail[t][size:, :size], small)
                trail[t] = trail[t][size:, size:] - dott(below, below)
                rest_inv[t] = rest_inv[t][size:, :] - dot(below, head)
    row = lax.broadcasted_iota(jnp.int32, (rank, rank), 0)
    col = lax.broadcasted_iota(jnp.int32, (rank, rank), 1)
    for t in range(tiles):
        inverse = jnp.concatenate(done[t], axis=0)
        basis_ref[t] = dott(rows_ref[:, t * rank:(t + 1) * rank], inverse) * scale
        lower = dott(gram_ref[t * rank:(t + 1) * rank, :], inverse)
        chol_ref[t] = jnp.where(row >= col, lower * (1.0 / scale), 0.0)


def couplings(tile_list, left, right, probe, xs, ys):
    panels, size, rank = left.shape
    rows = size // ys
    listed = tile_list.shape[1]
    number = xs * ys
    vmem = pl.BlockSpec(memory_space=pltpu.VMEM)
    dma = pltpu.SemaphoreType.DMA
    steps = ys // 2
    return pl.pallas_call(
        functools.partial(coupling_kernel, xs, ys),
        out_shape=jax.ShapeDtypeStruct((panels * rank, listed * rank), BF16),
        in_specs=[pl.BlockSpec(memory_space=pltpu.SMEM), vmem,
                  pl.BlockSpec(memory_space=pl.ANY), vmem],
        out_specs=vmem,
        scratch_shapes=[
            pltpu.VMEM((ys, rows, rank), BF16), pltpu.VMEM((ys, rows, rank), BF16),
            pltpu.VMEM((ys, rank, rank), BF16), pltpu.VMEM((ys, rank, rank), BF16),
            pltpu.VMEM((number, rows, rank), BF16), pltpu.VMEM((number, rows, rank), BF16),
            pltpu.VMEM((panels, 2, steps, rank, listed * rank), BF16),
            pltpu.VMEM((panels, 2, steps, rank, listed * rank), BF16),
            dma((panels,)), dma((panels, ys)), dma((panels, ys)), dma((panels, ys)),
            dma((panels, ys)), dma((panels, 2, ys)), dma((panels, ys)),
            dma((panels, number)), dma((panels, 2, steps)), dma((panels, 2, steps)),
        ],
        compiler_params=pltpu.CompilerParams(
            collective_id=0, has_side_effects=True, vmem_limit_bytes=40 * 2 ** 20),
        name="couplings",
    )(tile_list, left, right, probe)


def sums(left, coupling, zs):
    panels, size, rank = left.shape
    width = coupling.shape[1]
    rows = size // (zs * CORES)
    tiles = width // rank
    vmem = pl.BlockSpec(memory_space=pltpu.VMEM)
    dma = pltpu.SemaphoreType.DMA
    steps = zs // 2
    share = tiles * rank // CORES
    return pl.pallas_call(
        functools.partial(sum_kernel, zs),
        out_shape=(jax.ShapeDtypeStruct((rows, width), F32),
                   jax.ShapeDtypeStruct((tiles * rank, rank), F32)),
        in_specs=[vmem, vmem],
        out_specs=(vmem, vmem),
        scratch_shapes=[
            pltpu.VMEM((zs, rows, width), F32), pltpu.VMEM((zs, rows, width), F32),
            pltpu.VMEM((zs, rows, width), F32),
            pltpu.VMEM((2, 2, steps, rows, width // 2), BF16),
            pltpu.VMEM((2, 2, steps, rows, width // 2), BF16),
            pltpu.VMEM((tiles * rank, rank), F32), pltpu.VMEM((share, rank), F32),
            pltpu.VMEM((share, rank), F32), pltpu.VMEM((zs, share // zs, rank), F32),
            pltpu.VMEM((share // zs, rank), F32),
            pltpu.VMEM((share, rank), F32), pltpu.VMEM((share, rank), F32),
            dma((zs,)), dma((zs,)), dma((2, 2, steps)), dma((2, 2, steps)), dma, dma,
            dma((zs,)), dma((zs,)), dma((zs,)), dma((zs,)), dma, dma,
        ],
        compiler_params=pltpu.CompilerParams(
            collective_id=1, has_side_effects=True, vmem_limit_bytes=40 * 2 ** 20),
        name="sums",
    )(left, coupling)


def factors(rows, gram, scale):
    size, width = rows.shape
    rank = gram.shape[1]
    tiles = width // rank
    vmem = pl.BlockSpec(memory_space=pltpu.VMEM)
    return pl.pallas_call(
        functools.partial(factor_kernel, scale),
        out_shape=(jax.ShapeDtypeStruct((tiles, size, rank), F32),
                   jax.ShapeDtypeStruct((tiles, rank, rank), F32)),
        in_specs=[vmem, vmem],
        out_specs=(vmem, vmem),
        compiler_params=pltpu.CompilerParams(vmem_limit_bytes=40 * 2 ** 20),
        name="factors",
    )(rows, gram)


def solution(mesh):
    rows, depth = mesh.shape["rows"], mesh.shape["depth"]

    def on_device(left_factors, right_factors, probe_matrix, tile_list):
        left, right = left_factors[0], right_factors[0]
        scale = math.sqrt(float(left.shape[1]))
        coupling = couplings(tile_list, left, right, probe_matrix, XS, rows // XS)
        own_rows, gram = sums(left, coupling, depth // CORES)
        basis, lower = factors(own_rows, gram, scale)
        return basis[None], lower[None]

    in_specs = (P("rows", "depth", None, None), P("rows", "depth", None, None), P(), P())
    out_specs = (P("rows", None, "depth", None), P("rows", None, None, None))
    return jax.shard_map(
        on_device, mesh=mesh, in_specs=in_specs, out_specs=out_specs, check_vma=False
    )
```

```python
import functools
import math

import jax
import jax.numpy as jnp
from jax import lax
from jax.experimental import pallas as pl
from jax.experimental.pallas import tpu as pltpu
from jax.sharding import PartitionSpec as P

MESH = pl.DeviceIdType.MESH
F32 = jnp.float32
BF16 = jnp.bfloat16
XS = 4
CORES = 2
HIGHEST = lax.Precision.HIGHEST


def rcopy(src, dst, send_sem, recv_sem, device):
    return pltpu.make_async_remote_copy(
        src_ref=src, dst_ref=dst, send_sem=send_sem, recv_sem=recv_sem,
        device_id=device, device_id_type=MESH)


def tdot(a, b, precision=None):
    return lax.dot_general(a, b, (((0,), (0,)), ((), ())), precision=precision,
                           preferred_element_type=F32)


def update_kernel(xs, ys, zs, tile_ref, u_ref, v_ref, om_ref, rows_ref, gram_ref,
                  uv, om, vb0, vb1, ma, sa0, sa1, stage, rbuf, cpl,
                  xsend, xrecv, held, zstage, zbuf, gpart, gx, ghalf, gr, gall, gout,
                  u_sem, om_sem, own_sem, v_send, v_recv, m_send, m_recv,
                  s_send, f_send, s_recv, r_send, r_recv, x_send, x_recv,
                  z_send, z_recv, g_send, g_recv, a_send, a_recv, b_send, b_recv,
                  e_send, e_recv):
    vb, sa = (vb0, vb1), (sa0, sa1)
    panels, halves = 2, 2
    me, deep = lax.axis_index("rows"), lax.axis_index("depth")
    x, y = lax.div(me, ys), lax.rem(me, ys)
    z, c = lax.div(deep, CORES), lax.rem(deep, CORES)
    rows = vb0.shape[1]
    rank = ma.shape[2]
    listed = tile_ref.shape[1]
    per_half = listed // halves
    width = per_half * rank
    own_rows = rows_ref.shape[0]

    def at_x(dx):
        return {"rows": lax.rem(x + dx + xs, xs) * ys + y}

    def at_y(dy):
        return {"rows": x * ys + lax.rem(y + dy + ys, ys)}

    def at_z(dz):
        return {"depth": lax.rem(z + dz + zs, zs) * CORES + c}

    partner = {"depth": z * CORES + 1 - c}

    def wait_in(ref, sem):
        rcopy(ref, ref, sem, sem, partner).wait_recv()

    def wait_out(ref, sem):
        rcopy(ref, ref, sem, sem, partner).wait_send()

    sent = []

    def send(src, dst, send_sem, recv_sem, device):
        rcopy(src, dst, send_sem, recv_sem, device).start()
        sent.append((src, send_sem))

    def yat(dy):
        return lax.rem(y + dy + ys, ys)

    def zat(dz):
        return lax.rem(z + dz + zs, zs)

    u_copies = [pltpu.make_async_copy(u_ref.at[p], uv.at[p], u_sem.at[p]) for p in range(panels)]
    om_copy = pltpu.make_async_copy(om_ref, om, om_sem)
    om_copy.start()
    for copy in u_copies:
        copy.start()

    def v_rows(p, yd):
        return v_ref.at[p, pl.ds(pl.multiple_of(yd * rows, rows), rows), :]

    own = [pltpu.make_async_copy(v_rows(p, y), vb[p].at[y], own_sem.at[p]) for p in range(panels)]
    for copy in own:
        copy.start()
    barrier = pltpu.get_barrier_semaphore()
    greet = ([at_y(dy) for dy in range(1, ys)] + [at_x(1), at_x(-1)]
             + [at_z(dz) for dz in range(1, zs)] + [partner])
    for device in greet:
        pl.semaphore_signal(barrier, inc=1, device_id=device, device_id_type=MESH)
    om_copy.wait()
    for p in range(panels):
        u_copies[p].wait()
        ma[y, p] = tdot(uv[p], om[...]).astype(BF16)
    pl.semaphore_wait(barrier, len(greet))

    m_reach = {1: ys // 2, -1: ys - 1 - ys // 2}

    def send_m(source, go):
        send(ma.at[source], ma.at[source], m_send.at[source, (go + 1) // 2], m_recv.at[source],
             at_y(go))

    near = [0]
    for away in range(1, ys // 2 + 1):
        near += [-away, away] if 2 * away < ys else [-away]

    def sketch_block(p, s):
        yd = yat(near[s])
        if s == 0:
            own[p].wait()
        else:
            wait_in(vb[p].at[yd], v_recv.at[p, yd])
            if p == 0:
                wait_in(ma.at[yd], m_recv.at[yd])
                go = 1 if near[s] < 0 else -1
                if abs(near[s]) < m_reach[go]:
                    send_m(yd, go)
        block = x * ys + yd
        sa[p][block] = jnp.dot(vb[p][yd], ma[yd, p], preferred_element_type=F32).astype(BF16)
        for side, dx in enumerate((1, -1)):
            send(sa[p].at[block], sa[p].at[block], s_send.at[p, side, yd],
                 s_recv.at[p, block], at_x(dx))

    def forward(p, s):
        come, go = ((-1, 1), (1, -1))[p]
        yd = yat(near[s])
        block = lax.rem(x + come + xs, xs) * ys + yd
        wait_in(sa[p].at[block], s_recv.at[p, block])
        send(sa[p].at[block], sa[p].at[block], f_send.at[p, yd], s_recv.at[p, block], at_x(go))

    def rest_in(p):
        for yd in near:
            for dx in ((1, 2), (2, -1))[p]:
                block = lax.rem(x + dx + xs, xs) * ys + yat(yd)
                wait_in(sa[p].at[block], s_recv.at[p, block])

    def part(p, h, yd):
        row = x * ys + yd
        picked = jnp.concatenate(
            [sa[p][tile_ref[row, h * per_half + k]] for k in range(per_half)], axis=1)
        return tdot(vb[p][yd], picked)

    def chain(count, flip, side):
        return count // 2 if (side == 0) != (flip == 1) else count - 1 - count // 2

    def ring_step(p, h, s):
        for side in range(2):
            length = chain(ys, p, side)
            if s >= length:
                continue
            away = length - s
            term = part(p, h, yat(away if side == 0 else -away))
            if s > 0:
                wait_in(rbuf.at[p, h, side, s - 1], r_recv.at[p, h, side, s - 1])
                term = term + rbuf[p, h, side, s - 1].astype(F32)
            stage[p, h, side, s] = term.astype(BF16)
            send(stage.at[p, h, side, s], rbuf.at[p, h, side, s], r_send.at[p, h, side, s],
                 r_recv.at[p, h, side, s], at_y(1 if side == 0 else -1))

    def ring_end(p, h):
        term = part(p, h, y)
        for side in range(2):
            last = chain(ys, p, side) - 1
            wait_in(rbuf.at[p, h, side, last], r_recv.at[p, h, side, last])
            term = term + rbuf[p, h, side, last].astype(F32)
        cpl[h, p * rank:(p + 1) * rank, :] = term.astype(BF16)

    far = [zs // 2]
    for away in range(zs // 2 - 1, 0, -1):
        far += [away, -away]
    far.append(0)

    def term_rows(h, zd, cd):
        start = pl.multiple_of((zd * CORES + cd) * own_rows, own_rows)
        left = jnp.concatenate([uv[p, pl.ds(start, own_rows), :] for p in range(panels)], axis=1)
        return jnp.dot(left, cpl[h], preferred_element_type=F32)

    def give(h):
        for dz in far:
            zd = zat(dz)
            xsend[h, zd] = term_rows(h, zd, 1 - c).astype(BF16)
            send(xsend.at[h, zd], xrecv.at[h, zd], x_send.at[h, zd], x_recv.at[h, zd], partner)

    def take(h, dz):
        zd = zat(dz)
        mine = term_rows(h, zd, c)
        wait_in(xrecv.at[h, zd], x_recv.at[h, zd])
        held[h, zd] = mine + xrecv[h, zd].astype(F32)

    def held_tile(h, k, dz):
        return held[h, zat(dz), :, k * rank:(k + 1) * rank]

    def depth_step(h, s):
        for dz in far:
            if (abs(dz) == zs // 2 - s - 1 and dz != 0) or (s == 0 and abs(dz) == zs // 2):
                take(h, dz)
        for k in range(per_half):
            t = h * per_half + k
            for side in range(2):
                length = chain(zs, k % 2, side)
                if s >= length:
                    continue
                away = length - s
                if away == zs // 2:
                    term = held_tile(h, k, away)
                else:
                    term = held_tile(h, k, away if side == 0 else -away)
                if s > 0:
                    wait_in(zbuf.at[t, side, s - 1], z_recv.at[t, side, s - 1])
                    term = term + zbuf[t, side, s - 1].astype(F32)
                zstage[t, side, s] = term.astype(BF16)
                send(zstage.at[t, side, s], zbuf.at[t, side, s], z_send.at[t, side, s],
                     z_recv.at[t, side, s], at_z(1 if side == 0 else -1))

    def depth_end(h):
        take(h, 0)
        for k in range(per_half):
            t = h * per_half + k
            term = held_tile(h, k, 0)
            for side in range(2):
                last = chain(zs, k % 2, side) - 1
                wait_in(zbuf.at[t, side, last], z_recv.at[t, side, last])
                term = term + zbuf[t, side, last].astype(F32)
            rows_ref[:, t * rank:(t + 1) * rank] = term
            gpart[t] = tdot(term, term, HIGHEST)

    piece = rank // zs

    def piece_of(zd):
        return pl.ds(pl.multiple_of(zd * piece, piece), piece)

    def gram_swap(h):
        send(gpart.at[h * CORES + 1 - c], gx.at[h], g_send.at[h], g_recv.at[h], partner)

    def gram_spread(h):
        wait_in(gx.at[h], g_recv.at[h])
        ghalf[h] = gpart[h * CORES + c] + gx[h]
        for dz in near_z:
            send(ghalf.at[h, piece_of(zat(dz)), :], gr.at[h, z], a_send.at[h, zat(dz)],
                 a_recv.at[h, z], at_z(dz))
        gr[h, z] = ghalf[h, piece_of(z), :]

    def gram_gather(h):
        for dz in near_z:
            wait_in(gr.at[h, zat(dz)], a_recv.at[h, zat(dz)])
        total = gr[h, 0]
        for k in range(1, zs):
            total = total + gr[h, k]
        gall[h, piece_of(z), :] = total
        for dz in near_z:
            send(gall.at[h, piece_of(z), :], gall.at[h, piece_of(z), :], b_send.at[h, zat(dz)],
                 b_recv.at[h, z], at_z(dz))

    def gram_back(h):
        for dz in near_z:
            wait_in(gall.at[h, piece_of(zat(dz)), :], b_recv.at[h, zat(dz)])
        send(gall.at[h], gout.at[h], e_send.at[h], e_recv.at[h], partner)
        gram_ref[h * CORES + c] = gall[h]

    def gram_end(h):
        wait_in(gout.at[h], e_recv.at[h])
        gram_ref[h * CORES + 1 - c] = gout[h]

    near_z = [dz for dz in reversed(far) if dz != 0]

    turns = [(0, 0), (1, 0)]
    for s in range(1, ys, 2):
        turns += [(p, k) for p in range(panels) for k in (s, s + 1) if k < ys]
    queue = [(p, near[s]) for p, s in turns if s > 0]

    def send_next():
        if queue:
            p, dy = queue.pop(0)
            send(v_rows(p, yat(dy)), vb[p].at[y], v_send.at[p, yat(dy)], v_recv.at[p, y], at_y(dy))

    send_m(y, 1)
    send_m(y, -1)
    for _ in range(4):
        send_next()
    late = []
    for turn in turns:
        sketch_block(*turn)
        if turn[1] > 0:
            send_next()
        late.append(turn)
        if len(late) > 4:
            forward(*late.pop(0))
    for turn in late:
        forward(*turn)
    for p in range(panels):
        rest_in(p)
    for s in range(ys // 2):
        for p in range(panels):
            for h in range(halves):
                ring_step(p, h, s)
    for h in range(halves):
        for p in range(panels):
            ring_end(p, h)
        give(h)
    for s in range(zs // 2):
        for h in range(halves):
            depth_step(h, s)
    for stepper in (depth_end, gram_swap, gram_spread, gram_gather, gram_back, gram_end):
        for h in range(halves):
            stepper(h)
    for ref, sem in sent:
        wait_out(ref, sem)


def factor_kernel(scale, rows_ref, gram_ref, basis_ref, chol_ref):
    rank = gram_ref.shape[1]
    tiles = gram_ref.shape[0] // rank
    size = 128 // tiles
    lane = lax.broadcasted_iota(jnp.int32, (size, 128), 1)
    sub = lax.broadcasted_iota(jnp.int32, (size, 128), 0)
    first = (lane // size) * size
    unit = (lane - first == sub).astype(F32)

    def dott(a, b):
        return lax.dot_general(a, b, (((1,), (1,)), ((), ())), precision=HIGHEST,
                               preferred_element_type=F32)

    def dot(a, b):
        return jnp.dot(a, b, precision=HIGHEST, preferred_element_type=F32)

    trail = [gram_ref[t * rank:(t + 1) * rank, :] for t in range(tiles)]
    eye = (lax.broadcasted_iota(jnp.int32, (rank, rank), 0)
           == lax.broadcasted_iota(jnp.int32, (rank, rank), 1)).astype(F32)
    rest_inv = [eye] * tiles
    done = [[] for _ in range(tiles)]
    for b in range(rank // size):
        packed = jnp.concatenate([trail[t][:size, :size] for t in range(tiles)], axis=1)
        inv = unit
        pivots = jnp.ones((size, 128), F32)
        for k in range(size):
            column = jnp.take_along_axis(packed, first + k, axis=1)
            pivot = column[k:k + 1, :]
            times = jnp.where(sub > k, column / pivot, 0.0)
            pivots = jnp.where(sub == k, pivot, pivots)
            packed = packed - times * packed[k:k + 1, :]
            inv = inv - times * inv[k:k + 1, :]
        inv = inv * lax.rsqrt(pivots)
        for t in range(tiles):
            small = inv[:, t * size:(t + 1) * size]
            head = dot(small, rest_inv[t][:size, :])
            done[t].append(head)
            if (b + 1) * size < rank:
                below = dott(trail[t][size:, :size], small)
                trail[t] = trail[t][size:, size:] - dott(below, below)
                rest_inv[t] = rest_inv[t][size:, :] - dot(below, head)
    row = lax.broadcasted_iota(jnp.int32, (rank, rank), 0)
    col = lax.broadcasted_iota(jnp.int32, (rank, rank), 1)
    for t in range(tiles):
        inverse = jnp.concatenate(done[t], axis=0)
        basis_ref[t] = dott(rows_ref[:, t * rank:(t + 1) * rank], inverse) * scale
        lower = dott(gram_ref[t * rank:(t + 1) * rank, :], inverse)
        chol_ref[t] = jnp.where(row >= col, lower * (1.0 / scale), 0.0)


def updates(tile_list, left, right, probe, xs, ys, zs):
    panels, size, rank = left.shape
    rows, own_rows = size // ys, size // (zs * CORES)
    listed = tile_list.shape[1]
    number = xs * ys
    width = listed * rank // 2
    vmem = pl.BlockSpec(memory_space=pltpu.VMEM)
    hbm = pl.BlockSpec(memory_space=pl.ANY)
    dma = pltpu.SemaphoreType.DMA
    ysteps, zsteps = ys // 2, zs // 2
    return pl.pallas_call(
        functools.partial(update_kernel, xs, ys, zs),
        out_shape=(jax.ShapeDtypeStruct((own_rows, listed * rank), F32),
                   jax.ShapeDtypeStruct((listed, rank, rank), F32)),
        in_specs=[pl.BlockSpec(memory_space=pltpu.SMEM), hbm, hbm, hbm],
        out_specs=(vmem, vmem),
        scratch_shapes=[
            pltpu.VMEM((panels, size, rank), BF16), pltpu.VMEM((size, rank), BF16),
            pltpu.VMEM((ys, rows, rank), BF16), pltpu.VMEM((ys, rows, rank), BF16),
            pltpu.VMEM((ys, panels, rank, rank), BF16),
            pltpu.VMEM((number, rows, rank), BF16), pltpu.VMEM((number, rows, rank), BF16),
            pltpu.VMEM((panels, 2, 2, ysteps, rank, width), BF16),
            pltpu.VMEM((panels, 2, 2, ysteps, rank, width), BF16),
            pltpu.VMEM((2, panels * rank, width), BF16),
            pltpu.VMEM((2, zs, own_rows, width), BF16), pltpu.VMEM((2, zs, own_rows, width), BF16),
            pltpu.VMEM((2, zs, own_rows, width), F32),
            pltpu.VMEM((listed, 2, zsteps, own_rows, rank), BF16),
            pltpu.VMEM((listed, 2, zsteps, own_rows, rank), BF16),
            pltpu.VMEM((listed, rank, rank), F32), pltpu.VMEM((2, rank, rank), F32),
            pltpu.VMEM((2, rank, rank), F32), pltpu.VMEM((2, zs, rank // zs, rank), F32),
            pltpu.VMEM((2, rank, rank), F32), pltpu.VMEM((2, rank, rank), F32),
            dma((panels,)), dma, dma((panels,)), dma((panels, ys)), dma((panels, ys)),
            dma((ys, 2)), dma((ys,)), dma((panels, 2, ys)), dma((panels, ys)),
            dma((panels, number)), dma((panels, 2, 2, ysteps)), dma((panels, 2, 2, ysteps)),
            dma((2, zs)), dma((2, zs)), dma((listed, 2, zsteps)), dma((listed, 2, zsteps)),
            dma((2,)), dma((2,)), dma((2, zs)), dma((2, zs)), dma((2, zs)), dma((2, zs)),
            dma((2,)), dma((2,)),
        ],
        compiler_params=pltpu.CompilerParams(
            collective_id=0, has_side_effects=True, vmem_limit_bytes=56 * 2 ** 20),
        name="updates",
    )(tile_list, left, right, probe)


def factors(rows, gram, scale):
    size, width = rows.shape
    rank = gram.shape[1]
    tiles = width // rank
    vmem = pl.BlockSpec(memory_space=pltpu.VMEM)
    return pl.pallas_call(
        functools.partial(factor_kernel, scale),
        out_shape=(jax.ShapeDtypeStruct((tiles, size, rank), F32),
                   jax.ShapeDtypeStruct((tiles, rank, rank), F32)),
        in_specs=[vmem, vmem],
        out_specs=(vmem, vmem),
        compiler_params=pltpu.CompilerParams(vmem_limit_bytes=40 * 2 ** 20),
        name="factors",
    )(rows, gram)


def solution(mesh):
    rows, depth = mesh.shape["rows"], mesh.shape["depth"]

    def on_device(left_factors, right_factors, probe_matrix, tile_list):
        left, right = left_factors[0], right_factors[0]
        scale = math.sqrt(float(left.shape[1]))
        own_rows, gram = updates(tile_list, left, right, probe_matrix,
                                 XS, rows // XS, depth // CORES)
        gram = gram.reshape(-1, gram.shape[2])
        basis, lower = factors(own_rows, gram, scale)
        return basis[None], lower[None]

    in_specs = (P("rows", "depth", None, None), P("rows", "depth", None, None), P(), P())
    out_specs = (P("rows", None, "depth", None), P("rows", None, None, None))
    return jax.shard_map(
        on_device, mesh=mesh, in_specs=in_specs, out_specs=out_specs, check_vma=False
    )
```

```python
import functools
import math

import jax
import jax.numpy as jnp
from jax import lax
from jax.experimental import pallas as pl
from jax.experimental.pallas import tpu as pltpu
from jax.sharding import PartitionSpec as P

MESH = pl.DeviceIdType.MESH
F32 = jnp.float32
BF16 = jnp.bfloat16
XS = 4
CORES = 2
HIGHEST = lax.Precision.HIGHEST


def rcopy(src, dst, send_sem, recv_sem, device):
    return pltpu.make_async_remote_copy(
        src_ref=src, dst_ref=dst, send_sem=send_sem, recv_sem=recv_sem,
        device_id=device, device_id_type=MESH)


def tdot(a, b, precision=None):
    return lax.dot_general(a, b, (((0,), (0,)), ((), ())), precision=precision,
                           preferred_element_type=F32)


def update_kernel(xs, ys, zs, tile_ref, u_ref, v_ref, om_ref, rows_out, gram_out,
                  rows_ref, uv, om, vb0, vb1, ma, sa0, sa1, stage, rbuf, cpl,
                  xsend, xrecv, held, zstage, zbuf, gpart, gx, ghalf, gr, gall, gout,
                  u_sem, om_sem, own_sem, v_send, v_recv, m_send, m_recv,
                  s_send, f_send, s_recv, r_send, r_recv, x_send, x_recv,
                  z_send, z_recv, g_send, g_recv, a_send, a_recv, b_send, b_recv,
                  e_send, e_recv, rows_sem, tile_sem):
    vb, sa = (vb0, vb1), (sa0, sa1)
    panels, halves = 2, 2
    me, deep = lax.axis_index("rows"), lax.axis_index("depth")
    x, y = lax.div(me, ys), lax.rem(me, ys)
    z, c = lax.div(deep, CORES), lax.rem(deep, CORES)
    rows = vb0.shape[1]
    rank = ma.shape[2]
    listed = tile_ref.shape[0]
    per_half = listed // halves
    width = per_half * rank
    own_rows = rows_ref.shape[0]

    def at_x(dx):
        return {"rows": lax.rem(x + dx + xs, xs) * ys + y}

    def at_y(dy):
        return {"rows": x * ys + lax.rem(y + dy + ys, ys)}

    def at_z(dz):
        return {"depth": lax.rem(z + dz + zs, zs) * CORES + c}

    partner = {"depth": z * CORES + 1 - c}

    def wait_in(ref, sem):
        rcopy(ref, ref, sem, sem, partner).wait_recv()

    def wait_out(ref, sem):
        rcopy(ref, ref, sem, sem, partner).wait_send()

    sent = []

    def send(src, dst, send_sem, recv_sem, device):
        rcopy(src, dst, send_sem, recv_sem, device).start()
        sent.append((src, send_sem))

    def yat(dy):
        return lax.rem(y + dy + ys, ys)

    def zat(dz):
        return lax.rem(z + dz + zs, zs)

    u_copies = [pltpu.make_async_copy(u_ref.at[p], uv.at[p], u_sem.at[p]) for p in range(panels)]
    om_copy = pltpu.make_async_copy(om_ref, om, om_sem)
    om_copy.start()
    for copy in u_copies:
        copy.start()

    def v_rows(p, yd):
        return v_ref.at[p, pl.ds(pl.multiple_of(yd * rows, rows), rows), :]

    own = [pltpu.make_async_copy(v_rows(p, y), vb[p].at[y], own_sem.at[p]) for p in range(panels)]
    for copy in own:
        copy.start()
    barrier = pltpu.get_barrier_semaphore()
    greet = ([at_y(dy) for dy in range(1, ys)] + [at_x(1), at_x(-1)]
             + [at_z(dz) for dz in range(1, zs)] + [partner])
    for device in greet:
        pl.semaphore_signal(barrier, inc=1, device_id=device, device_id_type=MESH)
    om_copy.wait()
    for p in range(panels):
        u_copies[p].wait()
        ma[y, p] = tdot(uv[p], om[...]).astype(BF16)
    pl.semaphore_wait(barrier, len(greet))

    m_reach = {1: ys // 2, -1: ys - 1 - ys // 2}

    def send_m(source, go):
        send(ma.at[source], ma.at[source], m_send.at[source, (go + 1) // 2], m_recv.at[source],
             at_y(go))

    near = [0]
    for away in range(1, ys // 2 + 1):
        near += [-away, away] if 2 * away < ys else [-away]

    def sketch_block(p, s):
        yd = yat(near[s])
        if s == 0:
            own[p].wait()
        else:
            wait_in(vb[p].at[yd], v_recv.at[p, yd])
            if p == 0:
                wait_in(ma.at[yd], m_recv.at[yd])
                go = 1 if near[s] < 0 else -1
                if abs(near[s]) < m_reach[go]:
                    send_m(yd, go)
        block = x * ys + yd
        sa[p][block] = jnp.dot(vb[p][yd], ma[yd, p], preferred_element_type=F32).astype(BF16)
        for side, dx in enumerate((1, -1)):
            send(sa[p].at[block], sa[p].at[block], s_send.at[p, side, yd],
                 s_recv.at[p, block], at_x(dx))

    def forward(p, s):
        come, go = ((-1, 1), (1, -1))[p]
        yd = yat(near[s])
        block = lax.rem(x + come + xs, xs) * ys + yd
        wait_in(sa[p].at[block], s_recv.at[p, block])
        send(sa[p].at[block], sa[p].at[block], f_send.at[p, yd], s_recv.at[p, block], at_x(go))

    def rest_in(p):
        for yd in near:
            for dx in ((1, 2), (2, -1))[p]:
                block = lax.rem(x + dx + xs, xs) * ys + yat(yd)
                wait_in(sa[p].at[block], s_recv.at[p, block])

    def part(p, h, yd):
        row = x * ys + yd
        picked = jnp.concatenate(
            [sa[p][tile_ref[h * per_half + k, row]] for k in range(per_half)], axis=1)
        return tdot(vb[p][yd], picked)

    def chain(count, flip, side):
        return count // 2 if (side == 0) != (flip == 1) else count - 1 - count // 2

    def ring_step(p, h, s):
        for side in range(2):
            length = chain(ys, p, side)
            if s >= length:
                continue
            away = length - s
            term = part(p, h, yat(away if side == 0 else -away))
            if s > 0:
                wait_in(rbuf.at[p, h, side, s - 1], r_recv.at[p, h, side, s - 1])
                term = term + rbuf[p, h, side, s - 1].astype(F32)
            stage[p, h, side, s] = term.astype(BF16)
            send(stage.at[p, h, side, s], rbuf.at[p, h, side, s], r_send.at[p, h, side, s],
                 r_recv.at[p, h, side, s], at_y(1 if side == 0 else -1))

    def ring_end(p, h):
        term = part(p, h, y)
        for side in range(2):
            last = chain(ys, p, side) - 1
            wait_in(rbuf.at[p, h, side, last], r_recv.at[p, h, side, last])
            term = term + rbuf[p, h, side, last].astype(F32)
        cpl[h, p * rank:(p + 1) * rank, :] = term.astype(BF16)

    far = [zs // 2]
    for away in range(zs // 2 - 1, 0, -1):
        far += [away, -away]
    far.append(0)

    def term_rows(h, zd, cd):
        start = pl.multiple_of((zd * CORES + cd) * own_rows, own_rows)
        left = jnp.concatenate([uv[p, pl.ds(start, own_rows), :] for p in range(panels)], axis=1)
        return jnp.dot(left, cpl[h], preferred_element_type=F32)

    def give(h):
        for dz in far:
            zd = zat(dz)
            xsend[h, zd] = term_rows(h, zd, 1 - c).astype(BF16)
            send(xsend.at[h, zd], xrecv.at[h, zd], x_send.at[h, zd], x_recv.at[h, zd], partner)

    def take(h, dz):
        zd = zat(dz)
        mine = term_rows(h, zd, c)
        wait_in(xrecv.at[h, zd], x_recv.at[h, zd])
        held[h, zd] = mine + xrecv[h, zd].astype(F32)

    def held_tile(h, k, dz):
        return held[h, zat(dz), :, k * rank:(k + 1) * rank]

    def depth_step(h, s):
        for dz in far:
            if (abs(dz) == zs // 2 - s - 1 and dz != 0) or (s == 0 and abs(dz) == zs // 2):
                take(h, dz)
        for k in range(per_half):
            t = h * per_half + k
            for side in range(2):
                length = chain(zs, k % 2, side)
                if s >= length:
                    continue
                away = length - s
                if away == zs // 2:
                    term = held_tile(h, k, away)
                else:
                    term = held_tile(h, k, away if side == 0 else -away)
                if s > 0:
                    wait_in(zbuf.at[t, side, s - 1], z_recv.at[t, side, s - 1])
                    term = term + zbuf[t, side, s - 1].astype(F32)
                zstage[t, side, s] = term.astype(BF16)
                send(zstage.at[t, side, s], zbuf.at[t, side, s], z_send.at[t, side, s],
                     z_recv.at[t, side, s], at_z(1 if side == 0 else -1))

    def depth_end(h):
        take(h, 0)
        for k in range(per_half):
            t = h * per_half + k
            term = held_tile(h, k, 0)
            for side in range(2):
                last = chain(zs, k % 2, side) - 1
                wait_in(zbuf.at[t, side, last], z_recv.at[t, side, last])
                term = term + zbuf[t, side, last].astype(F32)
            rows_ref[:, t * rank:(t + 1) * rank] = term
            gpart[t] = tdot(term, term, HIGHEST)

    piece = rank // zs

    def piece_of(zd):
        return pl.ds(pl.multiple_of(zd * piece, piece), piece)

    rows_copy = pltpu.make_async_copy(rows_ref, rows_out, rows_sem)

    def tile_copy(ref, h, core):
        tile = h * CORES + core
        return pltpu.make_async_copy(ref.at[h], gram_out.at[tile], tile_sem.at[tile])

    def gram_swap(h):
        send(gpart.at[h * CORES + 1 - c], gx.at[h], g_send.at[h], g_recv.at[h], partner)

    def gram_spread(h):
        wait_in(gx.at[h], g_recv.at[h])
        ghalf[h] = gpart[h * CORES + c] + gx[h]
        for dz in near_z:
            send(ghalf.at[h, piece_of(zat(dz)), :], gr.at[h, z], a_send.at[h, zat(dz)],
                 a_recv.at[h, z], at_z(dz))
        gr[h, z] = ghalf[h, piece_of(z), :]

    def gram_gather(h):
        for dz in near_z:
            wait_in(gr.at[h, zat(dz)], a_recv.at[h, zat(dz)])
        total = gr[h, 0]
        for k in range(1, zs):
            total = total + gr[h, k]
        gall[h, piece_of(z), :] = total
        for dz in near_z:
            send(gall.at[h, piece_of(z), :], gall.at[h, piece_of(z), :], b_send.at[h, zat(dz)],
                 b_recv.at[h, z], at_z(dz))

    def gram_back(h):
        for dz in near_z:
            wait_in(gall.at[h, piece_of(zat(dz)), :], b_recv.at[h, zat(dz)])
        send(gall.at[h], gout.at[h], e_send.at[h], e_recv.at[h], partner)
        tile_copy(gall, h, c).start()

    def gram_end(h):
        wait_in(gout.at[h], e_recv.at[h])
        tile_copy(gout, h, 1 - c).start()

    near_z = [dz for dz in reversed(far) if dz != 0]

    turns = [(0, 0), (1, 0)]
    for s in range(1, ys, 2):
        turns += [(p, k) for p in range(panels) for k in (s, s + 1) if k < ys]
    queue = [(p, near[s]) for p, s in turns if s > 0]

    def send_next():
        if queue:
            p, dy = queue.pop(0)
            send(v_rows(p, yat(dy)), vb[p].at[y], v_send.at[p, yat(dy)], v_recv.at[p, y], at_y(dy))

    send_m(y, 1)
    send_m(y, -1)
    for _ in range(4):
        send_next()
    late = []
    for turn in turns:
        sketch_block(*turn)
        if turn[1] > 0:
            send_next()
        late.append(turn)
        if len(late) > 3:
            forward(*late.pop(0))
    for turn in late:
        forward(*turn)
    for p in range(panels):
        rest_in(p)
    for s in range(ys // 2):
        for h in range(halves):
            for p in range(panels):
                ring_step(p, h, s)
    for h in range(halves):
        for p in range(panels):
            ring_end(p, h)
        give(h)
        depth_step(h, 0)
    for s in range(1, zs // 2):
        for h in range(halves):
            depth_step(h, s)
    for h in range(halves):
        depth_end(h)
        gram_swap(h)
    rows_copy.start()
    for stepper in (gram_spread, gram_gather, gram_back, gram_end):
        for h in range(halves):
            stepper(h)
    for ref, sem in sent:
        wait_out(ref, sem)
    rows_copy.wait()
    for h in range(halves):
        tile_copy(gall, h, c).wait()
        tile_copy(gout, h, 1 - c).wait()


def eliminate(packed, size, wide):
    groups = size // 8
    sub = lax.broadcasted_iota(jnp.int32, (8, 128), 0)
    lane = lax.broadcasted_iota(jnp.int32, (8, 128), 1)
    head = (lane // size) * size
    left = [packed[8 * g:8 * g + 8, :] for g in range(groups)]
    inv = [(lane - head == sub + 8 * g).astype(F32) for g in range(groups)]
    scales = [None] * groups

    def spread(array, row):
        return jnp.broadcast_to(array[row:row + 1, :], (8, 128))

    for start in range(0, size, wide):
        top, row = start // 8, start % 8
        columns = [[jnp.take_along_axis(left[g], head + (start + j), axis=1)
                    for g in range(top, groups)] for j in range(wide)]
        small = [[spread(columns[j][0], row + i) for j in range(i + 1)] for i in range(wide)]
        pivot_rows = [spread(left[top], row + j) for j in range(wide)]
        inv_rows = [spread(inv[top], row + j) for j in range(wide)]
        times = [None] * wide
        for j in range(wide):
            root = lax.rsqrt(small[j][j])
            one = 1.0 / small[j][j]
            times[j] = [column * one for column in columns[j]]
            times[j][0] = jnp.where(sub > row + j, times[j][0], 0.0)
            old = jnp.ones((8, 128), F32) if scales[top] is None else scales[top]
            scales[top] = jnp.where(sub == row + j, root, old)
            for i in range(j + 1, wide):
                factor = small[i][j] * one
                pivot_rows[i] = pivot_rows[i] - factor * pivot_rows[j]
                inv_rows[i] = inv_rows[i] - factor * inv_rows[j]
                for k in range(i, wide):
                    small[k][i] = small[k][i] - factor * small[k][j]
                columns[i] = [a - b * small[i][j] for a, b in zip(columns[i], times[j])]
        for g in range(top, groups):
            for j in range(wide):
                left[g] = left[g] - times[j][g - top] * pivot_rows[j]
                inv[g] = inv[g] - times[j][g - top] * inv_rows[j]
    return jnp.concatenate([inv[g] * scales[g] for g in range(groups)], axis=0)


def factor_kernel(scale, rows_in, gram_in, basis_ref, chol_ref, rows_ref, gram_ref, sems):
    fetch_gram = pltpu.make_async_copy(gram_in, gram_ref, sems.at[0])
    fetch_rows = pltpu.make_async_copy(rows_in, rows_ref, sems.at[1])
    fetch_gram.start()
    fetch_rows.start()
    fetch_gram.wait()
    rank = gram_ref.shape[1]
    tiles = gram_ref.shape[0] // rank
    size = 128 // tiles

    def dott(a, b):
        return lax.dot_general(a, b, (((1,), (1,)), ((), ())), precision=HIGHEST,
                               preferred_element_type=F32)

    def dot(a, b):
        return jnp.dot(a, b, precision=HIGHEST, preferred_element_type=F32)

    trail = [gram_ref[t * rank:(t + 1) * rank, :] for t in range(tiles)]
    eye = (lax.broadcasted_iota(jnp.int32, (rank, rank), 0)
           == lax.broadcasted_iota(jnp.int32, (rank, rank), 1)).astype(F32)
    rest_inv = [eye] * tiles
    done = [[] for _ in range(tiles)]
    for b in range(rank // size):
        packed = jnp.concatenate([trail[t][:size, :size] for t in range(tiles)], axis=1)
        inv = eliminate(packed, size, 8)
        for t in range(tiles):
            small = inv[:, t * size:(t + 1) * size]
            head = dot(small, rest_inv[t][:size, :])
            done[t].append(head)
            if (b + 1) * size < rank:
                below = dott(trail[t][size:, :size], small)
                trail[t] = trail[t][size:, size:] - dott(below, below)
                rest_inv[t] = rest_inv[t][size:, :] - dot(below, head)
    row = lax.broadcasted_iota(jnp.int32, (rank, rank), 0)
    col = lax.broadcasted_iota(jnp.int32, (rank, rank), 1)
    fetch_rows.wait()
    for t in range(tiles):
        inverse = jnp.concatenate(done[t], axis=0)
        basis_ref[t] = dott(rows_ref[:, t * rank:(t + 1) * rank], inverse) * scale
        lower = dott(gram_ref[t * rank:(t + 1) * rank, :], inverse)
        chol_ref[t] = jnp.where(row >= col, lower * (1.0 / scale), 0.0)


def updates(tile_list, left, right, probe, xs, ys, zs):
    panels, size, rank = left.shape
    rows, own_rows = size // ys, size // (zs * CORES)
    listed = tile_list.shape[1]
    number = xs * ys
    width = listed * rank // 2
    vmem = pl.BlockSpec(memory_space=pltpu.VMEM)
    hbm = pl.BlockSpec(memory_space=pl.ANY)
    dma = pltpu.SemaphoreType.DMA
    ysteps, zsteps = ys // 2, zs // 2
    return pl.pallas_call(
        functools.partial(update_kernel, xs, ys, zs),
        out_shape=(jax.ShapeDtypeStruct((own_rows, listed * rank), F32),
                   jax.ShapeDtypeStruct((listed, rank, rank), F32)),
        in_specs=[pl.BlockSpec(memory_space=pltpu.SMEM), hbm, hbm, hbm],
        out_specs=(hbm, hbm),
        scratch_shapes=[
            pltpu.VMEM((own_rows, listed * rank), F32),
            pltpu.VMEM((panels, size, rank), BF16), pltpu.VMEM((size, rank), BF16),
            pltpu.VMEM((ys, rows, rank), BF16), pltpu.VMEM((ys, rows, rank), BF16),
            pltpu.VMEM((ys, panels, rank, rank), BF16),
            pltpu.VMEM((number, rows, rank), BF16), pltpu.VMEM((number, rows, rank), BF16),
            pltpu.VMEM((panels, 2, 2, ysteps, rank, width), BF16),
            pltpu.VMEM((panels, 2, 2, ysteps, rank, width), BF16),
            pltpu.VMEM((2, panels * rank, width), BF16),
            pltpu.VMEM((2, zs, own_rows, width), BF16), pltpu.VMEM((2, zs, own_rows, width), BF16),
            pltpu.VMEM((2, zs, own_rows, width), F32),
            pltpu.VMEM((listed, 2, zsteps, own_rows, rank), BF16),
            pltpu.VMEM((listed, 2, zsteps, own_rows, rank), BF16),
            pltpu.VMEM((listed, rank, rank), F32), pltpu.VMEM((2, rank, rank), F32),
            pltpu.VMEM((2, rank, rank), F32), pltpu.VMEM((2, zs, rank // zs, rank), F32),
            pltpu.VMEM((2, rank, rank), F32), pltpu.VMEM((2, rank, rank), F32),
            dma((panels,)), dma, dma((panels,)), dma((panels, ys)), dma((panels, ys)),
            dma((ys, 2)), dma((ys,)), dma((panels, 2, ys)), dma((panels, ys)),
            dma((panels, number)), dma((panels, 2, 2, ysteps)), dma((panels, 2, 2, ysteps)),
            dma((2, zs)), dma((2, zs)), dma((listed, 2, zsteps)), dma((listed, 2, zsteps)),
            dma((2,)), dma((2,)), dma((2, zs)), dma((2, zs)), dma((2, zs)), dma((2, zs)),
            dma((2,)), dma((2,)), dma, dma((listed,)),
        ],
        compiler_params=pltpu.CompilerParams(
            collective_id=0, has_side_effects=True, vmem_limit_bytes=56 * 2 ** 20),
        name="updates",
    )(jnp.transpose(tile_list), left, right, probe)


def factors(rows, gram, scale):
    size, width = rows.shape
    rank = gram.shape[1]
    tiles = width // rank
    vmem = pl.BlockSpec(memory_space=pltpu.VMEM)
    hbm = pl.BlockSpec(memory_space=pl.ANY)
    return pl.pallas_call(
        functools.partial(factor_kernel, scale),
        out_shape=(jax.ShapeDtypeStruct((tiles, size, rank), F32),
                   jax.ShapeDtypeStruct((tiles, rank, rank), F32)),
        in_specs=[hbm, hbm],
        out_specs=(vmem, vmem),
        scratch_shapes=[pltpu.VMEM((size, width), F32), pltpu.VMEM((tiles * rank, rank), F32),
                        pltpu.SemaphoreType.DMA((2,))],
        compiler_params=pltpu.CompilerParams(vmem_limit_bytes=60 * 2 ** 20),
        name="factors",
    )(rows, gram)


def solution(mesh):
    rows, depth = mesh.shape["rows"], mesh.shape["depth"]

    def on_device(left_factors, right_factors, probe_matrix, tile_list):
        left, right = left_factors[0], right_factors[0]
        scale = math.sqrt(float(left.shape[1]))
        own_rows, gram = updates(tile_list, left, right, probe_matrix,
                                 XS, rows // XS, depth // CORES)
        gram = gram.reshape(-1, gram.shape[2])
        basis, lower = factors(own_rows, gram, scale)
        return basis[None], lower[None]

    in_specs = (P("rows", "depth", None, None), P("rows", "depth", None, None), P(), P())
    out_specs = (P("rows", None, "depth", None), P("rows", None, None, None))
    return jax.shard_map(
        on_device, mesh=mesh, in_specs=in_specs, out_specs=out_specs, check_vma=False
    )
```

```python
import functools
import math

import jax
import jax.numpy as jnp
from jax import lax
from jax.experimental import pallas as pl
from jax.experimental.pallas import tpu as pltpu
from jax.sharding import PartitionSpec as P

MESH = pl.DeviceIdType.MESH
F32 = jnp.float32
BF16 = jnp.bfloat16
XS = 4
CORES = 2
HIGHEST = lax.Precision.HIGHEST


def rcopy(src, dst, send_sem, recv_sem, device):
    return pltpu.make_async_remote_copy(
        src_ref=src, dst_ref=dst, send_sem=send_sem, recv_sem=recv_sem,
        device_id=device, device_id_type=MESH)


def tdot(a, b, precision=None):
    return lax.dot_general(a, b, (((0,), (0,)), ((), ())), precision=precision,
                           preferred_element_type=F32)


def update_kernel(xs, ys, zs, tile_ref, u_ref, v_ref, om_ref, rows_out, gram_out,
                  rows_ref, uv, uo, om, vb0, vb1, ma, sa0, sa1, stage, rbuf, cpl,
                  cpo, held, zstage, zbuf, gpart, gx, ghalf, gr, gall, gout,
                  u_sem, om_sem, own_sem, v_send, v_recv, m_send, m_recv,
                  s_send, f_send, s_recv, r_send, r_recv, u_send, u_recv, x_send, x_recv,
                  z_send, z_recv, g_send, g_recv, a_send, a_recv, b_send, b_recv,
                  e_send, e_recv, rows_sem, tile_sem):
    vb, sa = (vb0, vb1), (sa0, sa1)
    panels, halves = 2, 2
    me, deep = lax.axis_index("rows"), lax.axis_index("depth")
    x, y = lax.div(me, ys), lax.rem(me, ys)
    z, c = lax.div(deep, CORES), lax.rem(deep, CORES)
    rows = vb0.shape[1]
    rank = ma.shape[2]
    listed = tile_ref.shape[0]
    per_half = listed // halves
    width = per_half * rank
    own_rows = rows_ref.shape[0]

    def at_x(dx):
        return {"rows": lax.rem(x + dx + xs, xs) * ys + y}

    def at_y(dy):
        return {"rows": x * ys + lax.rem(y + dy + ys, ys)}

    def at_z(dz):
        return {"depth": lax.rem(z + dz + zs, zs) * CORES + c}

    partner = {"depth": z * CORES + 1 - c}

    def wait_in(ref, sem):
        rcopy(ref, ref, sem, sem, partner).wait_recv()

    def wait_out(ref, sem):
        rcopy(ref, ref, sem, sem, partner).wait_send()

    sent = []

    def send(src, dst, send_sem, recv_sem, device):
        rcopy(src, dst, send_sem, recv_sem, device).start()
        sent.append((src, send_sem))

    def yat(dy):
        return lax.rem(y + dy + ys, ys)

    def zat(dz):
        return lax.rem(z + dz + zs, zs)

    u_copies = [pltpu.make_async_copy(u_ref.at[p], uv.at[p], u_sem.at[p]) for p in range(panels)]
    om_copy = pltpu.make_async_copy(om_ref, om, om_sem)
    om_copy.start()
    for copy in u_copies:
        copy.start()

    def v_rows(p, yd):
        return v_ref.at[p, pl.ds(pl.multiple_of(yd * rows, rows), rows), :]

    own = [pltpu.make_async_copy(v_rows(p, y), vb[p].at[y], own_sem.at[p]) for p in range(panels)]
    for copy in own:
        copy.start()
    barrier = pltpu.get_barrier_semaphore()
    greet = ([at_y(dy) for dy in range(1, ys)] + [at_x(1), at_x(-1)]
             + [at_z(dz) for dz in range(1, zs)] + [partner])
    for device in greet:
        pl.semaphore_signal(barrier, inc=1, device_id=device, device_id_type=MESH)
    om_copy.wait()
    for p in range(panels):
        u_copies[p].wait()
        ma[y, p] = tdot(uv[p].reshape(om.shape), om[...]).astype(BF16)
    pl.semaphore_wait(barrier, len(greet))

    m_reach = {1: ys // 2, -1: ys - 1 - ys // 2}

    def send_m(source, go):
        send(ma.at[source], ma.at[source], m_send.at[source, (go + 1) // 2], m_recv.at[source],
             at_y(go))

    near = [0]
    for away in range(1, ys // 2 + 1):
        near += [-away, away] if 2 * away < ys else [-away]

    def sketch_block(p, s):
        yd = yat(near[s])
        if s == 0:
            own[p].wait()
        else:
            wait_in(vb[p].at[yd], v_recv.at[p, yd])
            if p == 0:
                wait_in(ma.at[yd], m_recv.at[yd])
                go = 1 if near[s] < 0 else -1
                if abs(near[s]) < m_reach[go]:
                    send_m(yd, go)
        block = x * ys + yd
        sa[p][block] = jnp.dot(vb[p][yd], ma[yd, p], preferred_element_type=F32).astype(BF16)
        for side, dx in enumerate((1, -1)):
            send(sa[p].at[block], sa[p].at[block], s_send.at[p, side, yd],
                 s_recv.at[p, block], at_x(dx))

    def forward(p, s):
        come, go = ((-1, 1), (1, -1))[p]
        yd = yat(near[s])
        block = lax.rem(x + come + xs, xs) * ys + yd
        wait_in(sa[p].at[block], s_recv.at[p, block])
        send(sa[p].at[block], sa[p].at[block], f_send.at[p, yd], s_recv.at[p, block], at_x(go))

    def rest_in(p):
        for yd in near:
            for dx in ((1, 2), (2, -1))[p]:
                block = lax.rem(x + dx + xs, xs) * ys + yat(yd)
                wait_in(sa[p].at[block], s_recv.at[p, block])

    def part(p, h, yd):
        row = x * ys + yd
        picked = jnp.concatenate(
            [sa[p][tile_ref[h * per_half + k, row]] for k in range(per_half)], axis=1)
        return tdot(vb[p][yd], picked)

    def chain(count, flip, side):
        return count // 2 if (side == 0) != (flip == 1) else count - 1 - count // 2

    def ring_step(p, h, s):
        for side in range(2):
            length = chain(ys, p, side)
            if s >= length:
                continue
            away = length - s
            term = part(p, h, yat(away if side == 0 else -away))
            if s > 0:
                wait_in(rbuf.at[p, h, side, s - 1], r_recv.at[p, h, side, s - 1])
                term = term + rbuf[p, h, side, s - 1].astype(F32)
            stage[p, h, side, s] = term.astype(BF16)
            send(stage.at[p, h, side, s], rbuf.at[p, h, side, s], r_send.at[p, h, side, s],
                 r_recv.at[p, h, side, s], at_y(1 if side == 0 else -1))

    def ring_end(p, h):
        term = part(p, h, y)
        for side in range(2):
            last = chain(ys, p, side) - 1
            wait_in(rbuf.at[p, h, side, last], r_recv.at[p, h, side, last])
            term = term + rbuf[p, h, side, last].astype(F32)
        cpl[h, p * rank:(p + 1) * rank, :] = term.astype(BF16)

    far = [zs // 2]
    for away in range(zs // 2 - 1, 0, -1):
        far += [away, -away]
    far.append(0)

    def give(h):
        send(cpl.at[h], cpo.at[h], x_send.at[h], x_recv.at[h], partner)
        wait_in(cpo.at[h], x_recv.at[h])

    def take(h, dz):
        zd = zat(dz)
        left = jnp.concatenate([uv[p, zd, c] for p in range(panels)]
                               + [uo[p, zd] for p in range(panels)], axis=1)
        both = jnp.concatenate([cpl[h], cpo[h]], axis=0)
        held[h, zd] = jnp.dot(left, both, preferred_element_type=F32)

    def held_tile(h, k, dz):
        return held[h, zat(dz), :, k * rank:(k + 1) * rank]

    def depth_step(h, s):
        for dz in far:
            if (abs(dz) == zs // 2 - s - 1 and dz != 0) or (s == 0 and abs(dz) == zs // 2):
                take(h, dz)
        for k in range(per_half):
            t = h * per_half + k
            for side in range(2):
                length = chain(zs, k % 2, side)
                if s >= length:
                    continue
                away = length - s
                if away == zs // 2:
                    term = held_tile(h, k, away)
                else:
                    term = held_tile(h, k, away if side == 0 else -away)
                if s > 0:
                    wait_in(zbuf.at[t, side, s - 1], z_recv.at[t, side, s - 1])
                    term = term + zbuf[t, side, s - 1].astype(F32)
                zstage[t, side, s] = term.astype(BF16)
                send(zstage.at[t, side, s], zbuf.at[t, side, s], z_send.at[t, side, s],
                     z_recv.at[t, side, s], at_z(1 if side == 0 else -1))

    def depth_end(h):
        take(h, 0)
        for k in range(per_half):
            t = h * per_half + k
            term = held_tile(h, k, 0)
            for side in range(2):
                last = chain(zs, k % 2, side) - 1
                wait_in(zbuf.at[t, side, last], z_recv.at[t, side, last])
                term = term + zbuf[t, side, last].astype(F32)
            rows_ref[:, t * rank:(t + 1) * rank] = term
            gpart[t] = tdot(term, term, HIGHEST)

    piece = rank // zs

    def piece_of(zd):
        return pl.ds(pl.multiple_of(zd * piece, piece), piece)

    rows_copy = pltpu.make_async_copy(rows_ref, rows_out, rows_sem)

    def tile_copy(ref, h, core):
        tile = h * CORES + core
        return pltpu.make_async_copy(ref.at[h], gram_out.at[tile], tile_sem.at[tile])

    def gram_swap(h):
        send(gpart.at[h * CORES + 1 - c], gx.at[h], g_send.at[h], g_recv.at[h], partner)

    def gram_spread(h):
        wait_in(gx.at[h], g_recv.at[h])
        ghalf[h] = gpart[h * CORES + c] + gx[h]
        for dz in near_z:
            send(ghalf.at[h, piece_of(zat(dz)), :], gr.at[h, z], a_send.at[h, zat(dz)],
                 a_recv.at[h, z], at_z(dz))
        gr[h, z] = ghalf[h, piece_of(z), :]

    def gram_gather(h):
        for dz in near_z:
            wait_in(gr.at[h, zat(dz)], a_recv.at[h, zat(dz)])
        total = gr[h, 0]
        for k in range(1, zs):
            total = total + gr[h, k]
        gall[h, piece_of(z), :] = total
        for dz in near_z:
            send(gall.at[h, piece_of(z), :], gall.at[h, piece_of(z), :], b_send.at[h, zat(dz)],
                 b_recv.at[h, z], at_z(dz))

    def gram_back(h):
        for dz in near_z:
            wait_in(gall.at[h, piece_of(zat(dz)), :], b_recv.at[h, zat(dz)])
        send(gall.at[h], gout.at[h], e_send.at[h], e_recv.at[h], partner)
        tile_copy(gall, h, c).start()

    def gram_end(h):
        wait_in(gout.at[h], e_recv.at[h])
        tile_copy(gout, h, 1 - c).start()

    near_z = [dz for dz in reversed(far) if dz != 0]

    turns = [(0, 0), (1, 0)]
    for s in range(1, ys, 2):
        turns += [(p, k) for p in range(panels) for k in (s, s + 1) if k < ys]
    queue = [(p, near[s]) for p, s in turns if s > 0]

    def send_next():
        if queue:
            p, dy = queue.pop(0)
            send(v_rows(p, yat(dy)), vb[p].at[y], v_send.at[p, yat(dy)], v_recv.at[p, y], at_y(dy))

    send_m(y, 1)
    send_m(y, -1)
    for _ in range(4):
        send_next()
    send(u_ref.at[:, :, 1 - c], uo, u_send, u_recv, partner)
    late = []
    for turn in turns:
        sketch_block(*turn)
        if turn[1] > 0:
            send_next()
        late.append(turn)
        if len(late) > 3:
            forward(*late.pop(0))
    for turn in late:
        forward(*turn)
    for p in range(panels):
        rest_in(p)
    for s in range(ys // 2):
        for h in range(halves):
            for p in range(panels):
                ring_step(p, h, s)
    wait_in(uo, u_recv)
    for h in range(halves):
        for p in range(panels):
            ring_end(p, h)
        give(h)
        depth_step(h, 0)
    for s in range(1, zs // 2):
        for h in range(halves):
            depth_step(h, s)
    for h in range(halves):
        depth_end(h)
        gram_swap(h)
    rows_copy.start()
    for stepper in (gram_spread, gram_gather, gram_back, gram_end):
        for h in range(halves):
            stepper(h)
    for ref, sem in sent:
        wait_out(ref, sem)
    rows_copy.wait()
    for h in range(halves):
        tile_copy(gall, h, c).wait()
        tile_copy(gout, h, 1 - c).wait()


def eliminate(packed, size, wide):
    groups = size // 8
    sub = lax.broadcasted_iota(jnp.int32, (8, 128), 0)
    lane = lax.broadcasted_iota(jnp.int32, (8, 128), 1)
    head = (lane // size) * size
    left = [packed[8 * g:8 * g + 8, :] for g in range(groups)]
    inv = [(lane - head == sub + 8 * g).astype(F32) for g in range(groups)]
    scales = [None] * groups

    def spread(array, row):
        return jnp.broadcast_to(array[row:row + 1, :], (8, 128))

    for start in range(0, size, wide):
        top, row = start // 8, start % 8
        columns = [[jnp.take_along_axis(left[g], head + (start + j), axis=1)
                    for g in range(top, groups)] for j in range(wide)]
        small = [[spread(columns[j][0], row + i) for j in range(i + 1)] for i in range(wide)]
        pivot_rows = [spread(left[top], row + j) for j in range(wide)]
        inv_rows = [spread(inv[top], row + j) for j in range(wide)]
        times = [None] * wide
        for j in range(wide):
            root = lax.rsqrt(small[j][j])
            one = 1.0 / small[j][j]
            times[j] = [column * one for column in columns[j]]
            times[j][0] = jnp.where(sub > row + j, times[j][0], 0.0)
            old = jnp.ones((8, 128), F32) if scales[top] is None else scales[top]
            scales[top] = jnp.where(sub == row + j, root, old)
            for i in range(j + 1, wide):
                factor = small[i][j] * one
                pivot_rows[i] = pivot_rows[i] - factor * pivot_rows[j]
                inv_rows[i] = inv_rows[i] - factor * inv_rows[j]
                for k in range(i, wide):
                    small[k][i] = small[k][i] - factor * small[k][j]
                columns[i] = [a - b * small[i][j] for a, b in zip(columns[i], times[j])]
        for g in range(top, groups):
            for j in range(wide):
                left[g] = left[g] - times[j][g - top] * pivot_rows[j]
                inv[g] = inv[g] - times[j][g - top] * inv_rows[j]
    return jnp.concatenate([inv[g] * scales[g] for g in range(groups)], axis=0)


def factor_kernel(scale, rows_in, gram_in, basis_ref, chol_ref, rows_ref, gram_ref, sems):
    fetch_gram = pltpu.make_async_copy(gram_in, gram_ref, sems.at[0])
    fetch_rows = pltpu.make_async_copy(rows_in, rows_ref, sems.at[1])
    fetch_gram.start()
    fetch_rows.start()
    fetch_gram.wait()
    rank = gram_ref.shape[1]
    tiles = gram_ref.shape[0] // rank
    size = 128 // tiles

    def dott(a, b):
        return lax.dot_general(a, b, (((1,), (1,)), ((), ())), precision=HIGHEST,
                               preferred_element_type=F32)

    def dot(a, b):
        return jnp.dot(a, b, precision=HIGHEST, preferred_element_type=F32)

    trail = [gram_ref[t * rank:(t + 1) * rank, :] for t in range(tiles)]
    eye = (lax.broadcasted_iota(jnp.int32, (rank, rank), 0)
           == lax.broadcasted_iota(jnp.int32, (rank, rank), 1)).astype(F32)
    rest_inv = [eye] * tiles
    done = [[] for _ in range(tiles)]
    for b in range(rank // size):
        packed = jnp.concatenate([trail[t][:size, :size] for t in range(tiles)], axis=1)
        inv = eliminate(packed, size, 8)
        for t in range(tiles):
            small = inv[:, t * size:(t + 1) * size]
            head = dot(small, rest_inv[t][:size, :])
            done[t].append(head)
            if (b + 1) * size < rank:
                below = dott(trail[t][size:, :size], small)
                trail[t] = trail[t][size:, size:] - dott(below, below)
                rest_inv[t] = rest_inv[t][size:, :] - dot(below, head)
    row = lax.broadcasted_iota(jnp.int32, (rank, rank), 0)
    col = lax.broadcasted_iota(jnp.int32, (rank, rank), 1)
    fetch_rows.wait()
    for t in range(tiles):
        inverse = jnp.concatenate(done[t], axis=0)
        basis_ref[t] = dott(rows_ref[:, t * rank:(t + 1) * rank], inverse) * scale
        lower = dott(gram_ref[t * rank:(t + 1) * rank, :], inverse)
        chol_ref[t] = jnp.where(row >= col, lower * (1.0 / scale), 0.0)


def updates(tile_list, left, right, probe, xs, ys, zs):
    panels, size, rank = left.shape
    rows, own_rows = size // ys, size // (zs * CORES)
    listed = tile_list.shape[1]
    number = xs * ys
    width = listed * rank // 2
    vmem = pl.BlockSpec(memory_space=pltpu.VMEM)
    hbm = pl.BlockSpec(memory_space=pl.ANY)
    dma = pltpu.SemaphoreType.DMA
    ysteps, zsteps = ys // 2, zs // 2
    return pl.pallas_call(
        functools.partial(update_kernel, xs, ys, zs),
        out_shape=(jax.ShapeDtypeStruct((own_rows, listed * rank), F32),
                   jax.ShapeDtypeStruct((listed, rank, rank), F32)),
        in_specs=[pl.BlockSpec(memory_space=pltpu.SMEM), hbm, hbm, hbm],
        out_specs=(hbm, hbm),
        scratch_shapes=[
            pltpu.VMEM((own_rows, listed * rank), F32),
            pltpu.VMEM((panels, zs, CORES, own_rows, rank), BF16),
            pltpu.VMEM((panels, zs, own_rows, rank), BF16), pltpu.VMEM((size, rank), BF16),
            pltpu.VMEM((ys, rows, rank), BF16), pltpu.VMEM((ys, rows, rank), BF16),
            pltpu.VMEM((ys, panels, rank, rank), BF16),
            pltpu.VMEM((number, rows, rank), BF16), pltpu.VMEM((number, rows, rank), BF16),
            pltpu.VMEM((panels, 2, 2, ysteps, rank, width), BF16),
            pltpu.VMEM((panels, 2, 2, ysteps, rank, width), BF16),
            pltpu.VMEM((2, panels * rank, width), BF16),
            pltpu.VMEM((2, panels * rank, width), BF16),
            pltpu.VMEM((2, zs, own_rows, width), F32),
            pltpu.VMEM((listed, 2, zsteps, own_rows, rank), BF16),
            pltpu.VMEM((listed, 2, zsteps, own_rows, rank), BF16),
            pltpu.VMEM((listed, rank, rank), F32), pltpu.VMEM((2, rank, rank), F32),
            pltpu.VMEM((2, rank, rank), F32), pltpu.VMEM((2, zs, rank // zs, rank), F32),
            pltpu.VMEM((2, rank, rank), F32), pltpu.VMEM((2, rank, rank), F32),
            dma((panels,)), dma, dma((panels,)), dma((panels, ys)), dma((panels, ys)),
            dma((ys, 2)), dma((ys,)), dma((panels, 2, ys)), dma((panels, ys)),
            dma((panels, number)), dma((panels, 2, 2, ysteps)), dma((panels, 2, 2, ysteps)),
            dma, dma, dma((2,)), dma((2,)), dma((listed, 2, zsteps)), dma((listed, 2, zsteps)),
            dma((2,)), dma((2,)), dma((2, zs)), dma((2, zs)), dma((2, zs)), dma((2, zs)),
            dma((2,)), dma((2,)), dma, dma((listed,)),
        ],
        compiler_params=pltpu.CompilerParams(
            collective_id=0, has_side_effects=True, vmem_limit_bytes=56 * 2 ** 20),
        name="updates",
    )(jnp.transpose(tile_list), left.reshape(panels, zs, CORES, own_rows, rank), right, probe)


def factors(rows, gram, scale):
    size, width = rows.shape
    rank = gram.shape[1]
    tiles = width // rank
    vmem = pl.BlockSpec(memory_space=pltpu.VMEM)
    hbm = pl.BlockSpec(memory_space=pl.ANY)
    return pl.pallas_call(
        functools.partial(factor_kernel, scale),
        out_shape=(jax.ShapeDtypeStruct((tiles, size, rank), F32),
                   jax.ShapeDtypeStruct((tiles, rank, rank), F32)),
        in_specs=[hbm, hbm],
        out_specs=(vmem, vmem),
        scratch_shapes=[pltpu.VMEM((size, width), F32), pltpu.VMEM((tiles * rank, rank), F32),
                        pltpu.SemaphoreType.DMA((2,))],
        compiler_params=pltpu.CompilerParams(vmem_limit_bytes=60 * 2 ** 20),
        name="factors",
    )(rows, gram)


def solution(mesh):
    rows, depth = mesh.shape["rows"], mesh.shape["depth"]

    def on_device(left_factors, right_factors, probe_matrix, tile_list):
        left, right = left_factors[0], right_factors[0]
        scale = math.sqrt(float(left.shape[1]))
        own_rows, gram = updates(tile_list, left, right, probe_matrix,
                                 XS, rows // XS, depth // CORES)
        gram = gram.reshape(-1, gram.shape[2])
        basis, lower = factors(own_rows, gram, scale)
        return basis[None], lower[None]

    in_specs = (P("rows", "depth", None, None), P("rows", "depth", None, None), P(), P())
    out_specs = (P("rows", None, "depth", None), P("rows", None, None, None))
    return jax.shard_map(
        on_device, mesh=mesh, in_specs=in_specs, out_specs=out_specs, check_vma=False
    )
```

```python
import functools
import math

import jax
import jax.numpy as jnp
from jax import lax
from jax.experimental import pallas as pl
from jax.experimental.pallas import tpu as pltpu
from jax.sharding import PartitionSpec as P

MESH = pl.DeviceIdType.MESH
F32 = jnp.float32
BF16 = jnp.bfloat16
XS = 4
CORES = 2
HIGHEST = lax.Precision.HIGHEST


def rcopy(src, dst, send_sem, recv_sem, device):
    return pltpu.make_async_remote_copy(
        src_ref=src, dst_ref=dst, send_sem=send_sem, recv_sem=recv_sem,
        device_id=device, device_id_type=MESH)


def tdot(a, b, precision=None):
    return lax.dot_general(a, b, (((0,), (0,)), ((), ())), precision=precision,
                           preferred_element_type=F32)


def update_kernel(xs, ys, zs, tile_ref, u_ref, v_ref, om_ref, rows_out, gram_out,
                  rows_ref, uv, uo, om, vb0, vb1, ma, sa0, sa1, stage, rbuf, cpl,
                  cpo, held, zstage, zbuf, gpart, gx, ghalf, gr, gall, gout,
                  u_sem, om_sem, own_sem, v_send, v_recv, m_send, m_recv,
                  s_send, f_send, s_recv, r_send, r_recv, u_send, u_recv, x_send, x_recv,
                  z_send, z_recv, g_send, g_recv, a_send, a_recv, b_send, b_recv,
                  e_send, e_recv, rows_sem, tile_sem):
    vb, sa = (vb0, vb1), (sa0, sa1)
    panels, halves = 2, 2
    me, deep = lax.axis_index("rows"), lax.axis_index("depth")
    x, y = lax.div(me, ys), lax.rem(me, ys)
    z, c = lax.div(deep, CORES), lax.rem(deep, CORES)
    rows = vb0.shape[1]
    rank = ma.shape[2]
    listed = tile_ref.shape[0]
    per_half = listed // halves
    width = per_half * rank
    own_rows = rows_ref.shape[0]

    def at_x(dx):
        return {"rows": lax.rem(x + dx + xs, xs) * ys + y}

    def at_y(dy):
        return {"rows": x * ys + lax.rem(y + dy + ys, ys)}

    def at_z(dz):
        return {"depth": lax.rem(z + dz + zs, zs) * CORES + c}

    partner = {"depth": z * CORES + 1 - c}

    def wait_in(ref, sem):
        rcopy(ref, ref, sem, sem, partner).wait_recv()

    def wait_out(ref, sem):
        rcopy(ref, ref, sem, sem, partner).wait_send()

    sent = []

    def send(src, dst, send_sem, recv_sem, device):
        rcopy(src, dst, send_sem, recv_sem, device).start()
        sent.append((src, send_sem))

    def yat(dy):
        return lax.rem(y + dy + ys, ys)

    def zat(dz):
        return lax.rem(z + dz + zs, zs)

    u_copies = [pltpu.make_async_copy(u_ref.at[p], uv.at[p], u_sem.at[p]) for p in range(panels)]
    om_copy = pltpu.make_async_copy(om_ref, om, om_sem)
    om_copy.start()
    for copy in u_copies:
        copy.start()

    def v_rows(p, yd):
        return v_ref.at[p, pl.ds(pl.multiple_of(yd * rows, rows), rows), :]

    own = [pltpu.make_async_copy(v_rows(p, y), vb[p].at[y], own_sem.at[p]) for p in range(panels)]
    for copy in own:
        copy.start()
    barrier = pltpu.get_barrier_semaphore()
    greet = ([at_y(dy) for dy in range(1, ys)] + [at_x(1), at_x(-1)]
             + [at_z(dz) for dz in range(1, zs)] + [partner])
    for device in greet:
        pl.semaphore_signal(barrier, inc=1, device_id=device, device_id_type=MESH)
    om_copy.wait()
    for p in range(panels):
        u_copies[p].wait()
        ma[y, p] = tdot(uv[p].reshape(om.shape), om[...]).astype(BF16)
    pl.semaphore_wait(barrier, len(greet))

    m_reach = {1: ys // 2, -1: ys - 1 - ys // 2}

    def send_m(source, go):
        send(ma.at[source], ma.at[source], m_send.at[source, (go + 1) // 2], m_recv.at[source],
             at_y(go))

    near = [0]
    for away in range(1, ys // 2 + 1):
        near += [-away, away] if 2 * away < ys else [-away]

    def sketch_block(p, s):
        yd = yat(near[s])
        if s == 0:
            own[p].wait()
        else:
            wait_in(vb[p].at[yd], v_recv.at[p, yd])
            if p == 0:
                wait_in(ma.at[yd], m_recv.at[yd])
                go = 1 if near[s] < 0 else -1
                if abs(near[s]) < m_reach[go]:
                    send_m(yd, go)
        block = x * ys + yd
        sa[p][block] = jnp.dot(vb[p][yd], ma[yd, p], preferred_element_type=F32).astype(BF16)
        for side, dx in enumerate((1, -1)):
            send(sa[p].at[block], sa[p].at[block], s_send.at[p, side, yd],
                 s_recv.at[p, block], at_x(dx))

    def forward(p, s):
        come, go = ((-1, 1), (1, -1))[p]
        yd = yat(near[s])
        block = lax.rem(x + come + xs, xs) * ys + yd
        wait_in(sa[p].at[block], s_recv.at[p, block])
        send(sa[p].at[block], sa[p].at[block], f_send.at[p, yd], s_recv.at[p, block], at_x(go))

    def rest_in(p):
        for yd in near:
            for dx in ((1, 2), (2, -1))[p]:
                block = lax.rem(x + dx + xs, xs) * ys + yat(yd)
                wait_in(sa[p].at[block], s_recv.at[p, block])

    def part(p, h, yd):
        row = x * ys + yd
        picked = jnp.concatenate(
            [sa[p][tile_ref[h * per_half + k, row]] for k in range(per_half)], axis=1)
        return tdot(vb[p][yd], picked)

    def chain(count, flip, side):
        return count // 2 if (side == 0) != (flip == 1) else count - 1 - count // 2

    def ring_step(p, h, s):
        for side in range(2):
            length = chain(ys, p, side)
            if s >= length:
                continue
            away = length - s
            term = part(p, h, yat(away if side == 0 else -away))
            if s > 0:
                wait_in(rbuf.at[p, h, side, s - 1], r_recv.at[p, h, side, s - 1])
                term = term + rbuf[p, h, side, s - 1].astype(F32)
            stage[p, h, side, s] = term.astype(BF16)
            send(stage.at[p, h, side, s], rbuf.at[p, h, side, s], r_send.at[p, h, side, s],
                 r_recv.at[p, h, side, s], at_y(1 if side == 0 else -1))

    def ring_end(p, h):
        term = part(p, h, y)
        for side in range(2):
            last = chain(ys, p, side) - 1
            wait_in(rbuf.at[p, h, side, last], r_recv.at[p, h, side, last])
            term = term + rbuf[p, h, side, last].astype(F32)
        cpl[h, p * rank:(p + 1) * rank, :] = term.astype(BF16)

    far = [zs // 2]
    for away in range(zs // 2 - 1, 0, -1):
        far += [away, -away]
    far.append(0)

    def give(h):
        send(cpl.at[h], cpo.at[h], x_send.at[h], x_recv.at[h], partner)
        wait_in(cpo.at[h], x_recv.at[h])

    def take(h, dz):
        zd = zat(dz)
        left = jnp.concatenate([uv[p, zd, c] for p in range(panels)]
                               + [uo[p, zd] for p in range(panels)], axis=1)
        both = jnp.concatenate([cpl[h], cpo[h]], axis=0)
        held[h, zd] = jnp.dot(left, both, preferred_element_type=F32)

    def held_tile(h, k, dz):
        return held[h, zat(dz), :, k * rank:(k + 1) * rank]

    def depth_step(h, s):
        for dz in far:
            if (abs(dz) == zs // 2 - s - 1 and dz != 0) or (s == 0 and abs(dz) == zs // 2):
                take(h, dz)
        for k in range(per_half):
            t = h * per_half + k
            for side in range(2):
                length = chain(zs, k % 2, side)
                if s >= length:
                    continue
                away = length - s
                if away == zs // 2:
                    term = held_tile(h, k, away)
                else:
                    term = held_tile(h, k, away if side == 0 else -away)
                if s > 0:
                    wait_in(zbuf.at[t, side, s - 1], z_recv.at[t, side, s - 1])
                    term = term + zbuf[t, side, s - 1].astype(F32)
                zstage[t, side, s] = term.astype(BF16)
                send(zstage.at[t, side, s], zbuf.at[t, side, s], z_send.at[t, side, s],
                     z_recv.at[t, side, s], at_z(1 if side == 0 else -1))

    def depth_end(h):
        take(h, 0)
        for k in range(per_half):
            t = h * per_half + k
            term = held_tile(h, k, 0)
            for side in range(2):
                last = chain(zs, k % 2, side) - 1
                wait_in(zbuf.at[t, side, last], z_recv.at[t, side, last])
                term = term + zbuf[t, side, last].astype(F32)
            rows_ref[:, t * rank:(t + 1) * rank] = term
            gpart[t] = tdot(term, term, HIGHEST)

    piece = rank // zs

    def piece_of(zd):
        return pl.ds(pl.multiple_of(zd * piece, piece), piece)

    rows_copy = pltpu.make_async_copy(rows_ref, rows_out, rows_sem)

    def tile_copy(ref, h, core):
        tile = h * CORES + core
        return pltpu.make_async_copy(ref.at[h], gram_out.at[tile], tile_sem.at[tile])

    def gram_swap(h):
        send(gpart.at[h * CORES + 1 - c], gx.at[h], g_send.at[h], g_recv.at[h], partner)

    def gram_spread(h):
        wait_in(gx.at[h], g_recv.at[h])
        ghalf[h] = gpart[h * CORES + c] + gx[h]
        for dz in near_z:
            send(ghalf.at[h, piece_of(zat(dz)), :], gr.at[h, z], a_send.at[h, zat(dz)],
                 a_recv.at[h, z], at_z(dz))
        gr[h, z] = ghalf[h, piece_of(z), :]

    def gram_gather(h):
        for dz in near_z:
            wait_in(gr.at[h, zat(dz)], a_recv.at[h, zat(dz)])
        total = gr[h, 0]
        for k in range(1, zs):
            total = total + gr[h, k]
        gall[h, piece_of(z), :] = total
        for dz in near_z:
            send(gall.at[h, piece_of(z), :], gall.at[h, piece_of(z), :], b_send.at[h, zat(dz)],
                 b_recv.at[h, z], at_z(dz))

    def gram_back(h):
        for dz in near_z:
            wait_in(gall.at[h, piece_of(zat(dz)), :], b_recv.at[h, zat(dz)])
        send(gall.at[h], gout.at[h], e_send.at[h], e_recv.at[h], partner)
        tile_copy(gall, h, c).start()

    def gram_end(h):
        wait_in(gout.at[h], e_recv.at[h])
        tile_copy(gout, h, 1 - c).start()

    near_z = [dz for dz in reversed(far) if dz != 0]

    turns = [(0, 0), (1, 0)]
    for s in range(1, ys, 2):
        turns += [(p, k) for p in range(panels) for k in (s, s + 1) if k < ys]
    queue = [(p, near[s]) for p, s in turns if s > 0]

    def send_next():
        if queue:
            p, dy = queue.pop(0)
            send(v_rows(p, yat(dy)), vb[p].at[y], v_send.at[p, yat(dy)], v_recv.at[p, y], at_y(dy))

    send_m(y, 1)
    send_m(y, -1)
    for _ in range(4):
        send_next()
    send(u_ref.at[:, :, 1 - c], uo, u_send, u_recv, partner)
    late = []
    for turn in turns:
        sketch_block(*turn)
        if turn[1] > 0:
            send_next()
        late.append(turn)
        if len(late) > 3:
            forward(*late.pop(0))
    for turn in late:
        forward(*turn)
    for p in range(panels):
        rest_in(p)
    for s in range(ys // 2):
        for h in range(halves):
            for p in range(panels):
                ring_step(p, h, s)
    wait_in(uo, u_recv)
    for h in range(halves):
        for p in range(panels):
            ring_end(p, h)
        give(h)
        depth_step(h, 0)
    for s in range(1, zs // 2):
        for h in range(halves):
            depth_step(h, s)
    for h in range(halves):
        depth_end(h)
        gram_swap(h)
    rows_copy.start()
    for stepper in (gram_spread, gram_gather, gram_back, gram_end):
        for h in range(halves):
            stepper(h)
    for ref, sem in sent:
        wait_out(ref, sem)
    rows_copy.wait()
    for h in range(halves):
        tile_copy(gall, h, c).wait()
        tile_copy(gout, h, 1 - c).wait()


def eliminate(packed, size, wide):
    groups = size // 8
    sub = lax.broadcasted_iota(jnp.int32, (8, 128), 0)
    lane = lax.broadcasted_iota(jnp.int32, (8, 128), 1)
    head = (lane // size) * size
    left = [packed[8 * g:8 * g + 8, :] for g in range(groups)]
    inv = [(lane - head == sub + 8 * g).astype(F32) for g in range(groups)]
    scales = [None] * groups

    def spread(array, row):
        return jnp.broadcast_to(array[row:row + 1, :], (8, 128))

    for start in range(0, size, wide):
        top, row = start // 8, start % 8
        columns = [[jnp.take_along_axis(left[g], head + (start + j), axis=1)
                    for g in range(top, groups)] for j in range(wide)]
        small = [[spread(columns[j][0], row + i) for j in range(i + 1)] for i in range(wide)]
        pivot_rows = [spread(left[top], row + j) for j in range(wide)]
        inv_rows = [spread(inv[top], row + j) for j in range(wide)]
        times = [None] * wide
        for j in range(wide):
            root = lax.rsqrt(small[j][j])
            one = 1.0 / small[j][j]
            times[j] = [column * one for column in columns[j]]
            times[j][0] = jnp.where(sub > row + j, times[j][0], 0.0)
            old = jnp.ones((8, 128), F32) if scales[top] is None else scales[top]
            scales[top] = jnp.where(sub == row + j, root, old)
            for i in range(j + 1, wide):
                factor = small[i][j] * one
                pivot_rows[i] = pivot_rows[i] - factor * pivot_rows[j]
                inv_rows[i] = inv_rows[i] - factor * inv_rows[j]
                for k in range(i, wide):
                    small[k][i] = small[k][i] - factor * small[k][j]
                columns[i] = [a - b * small[i][j] for a, b in zip(columns[i], times[j])]
        for g in range(top, groups):
            for j in range(wide):
                left[g] = left[g] - times[j][g - top] * pivot_rows[j]
                inv[g] = inv[g] - times[j][g - top] * inv_rows[j]
    return jnp.concatenate([inv[g] * scales[g] for g in range(groups)], axis=0)


def dot_halves(a, b):
    a_high, b_high = a.astype(BF16), b.astype(BF16)
    a_low = (a - a_high.astype(F32)).astype(BF16)
    b_low = (b - b_high.astype(F32)).astype(BF16)
    return lax.dot_general(
        jnp.concatenate([a_high, a_high, a_low], axis=1),
        jnp.concatenate([b_high, b_low, b_high], axis=1),
        (((1,), (1,)), ((), ())), preferred_element_type=F32)


def factor_kernel(scale, rows_in, gram_in, basis_ref, chol_ref, rows_ref, gram_ref, sems):
    fetch_gram = pltpu.make_async_copy(gram_in, gram_ref, sems.at[0])
    fetch_rows = pltpu.make_async_copy(rows_in, rows_ref, sems.at[1])
    fetch_gram.start()
    fetch_rows.start()
    fetch_gram.wait()
    rank = gram_ref.shape[1]
    tiles = gram_ref.shape[0] // rank
    size = 128 // tiles

    def dott(a, b):
        return lax.dot_general(a, b, (((1,), (1,)), ((), ())), precision=HIGHEST,
                               preferred_element_type=F32)

    def dot(a, b):
        return jnp.dot(a, b, precision=HIGHEST, preferred_element_type=F32)

    trail = [gram_ref[t * rank:(t + 1) * rank, :] for t in range(tiles)]
    eye = (lax.broadcasted_iota(jnp.int32, (rank, rank), 0)
           == lax.broadcasted_iota(jnp.int32, (rank, rank), 1)).astype(F32)
    rest_inv = [eye] * tiles
    done = [[] for _ in range(tiles)]
    for b in range(rank // size):
        packed = jnp.concatenate([trail[t][:size, :size] for t in range(tiles)], axis=1)
        inv = eliminate(packed, size, 8)
        for t in range(tiles):
            small = inv[:, t * size:(t + 1) * size]
            head = dot(small, rest_inv[t][:size, :])
            done[t].append(head)
            if (b + 1) * size < rank:
                below = dott(trail[t][size:, :size], small)
                trail[t] = trail[t][size:, size:] - dott(below, below)
                rest_inv[t] = rest_inv[t][size:, :] - dot(below, head)
    row = lax.broadcasted_iota(jnp.int32, (rank, rank), 0)
    col = lax.broadcasted_iota(jnp.int32, (rank, rank), 1)
    fetch_rows.wait()
    for t in range(tiles):
        inverse = jnp.concatenate(done[t], axis=0)
        basis_ref[t] = dot_halves(rows_ref[:, t * rank:(t + 1) * rank], inverse) * scale
        lower = dot_halves(gram_ref[t * rank:(t + 1) * rank, :], inverse)
        chol_ref[t] = jnp.where(row >= col, lower * (1.0 / scale), 0.0)


def updates(tile_list, left, right, probe, xs, ys, zs):
    panels, size, rank = left.shape
    rows, own_rows = size // ys, size // (zs * CORES)
    listed = tile_list.shape[1]
    number = xs * ys
    width = listed * rank // 2
    vmem = pl.BlockSpec(memory_space=pltpu.VMEM)
    hbm = pl.BlockSpec(memory_space=pl.ANY)
    dma = pltpu.SemaphoreType.DMA
    ysteps, zsteps = ys // 2, zs // 2
    return pl.pallas_call(
        functools.partial(update_kernel, xs, ys, zs),
        out_shape=(jax.ShapeDtypeStruct((own_rows, listed * rank), F32),
                   jax.ShapeDtypeStruct((listed, rank, rank), F32)),
        in_specs=[pl.BlockSpec(memory_space=pltpu.SMEM), hbm, hbm, hbm],
        out_specs=(hbm, hbm),
        scratch_shapes=[
            pltpu.VMEM((own_rows, listed * rank), F32),
            pltpu.VMEM((panels, zs, CORES, own_rows, rank), BF16),
            pltpu.VMEM((panels, zs, own_rows, rank), BF16), pltpu.VMEM((size, rank), BF16),
            pltpu.VMEM((ys, rows, rank), BF16), pltpu.VMEM((ys, rows, rank), BF16),
            pltpu.VMEM((ys, panels, rank, rank), BF16),
            pltpu.VMEM((number, rows, rank), BF16), pltpu.VMEM((number, rows, rank), BF16),
            pltpu.VMEM((panels, 2, 2, ysteps, rank, width), BF16),
            pltpu.VMEM((panels, 2, 2, ysteps, rank, width), BF16),
            pltpu.VMEM((2, panels * rank, width), BF16),
            pltpu.VMEM((2, panels * rank, width), BF16),
            pltpu.VMEM((2, zs, own_rows, width), F32),
            pltpu.VMEM((listed, 2, zsteps, own_rows, rank), BF16),
            pltpu.VMEM((listed, 2, zsteps, own_rows, rank), BF16),
            pltpu.VMEM((listed, rank, rank), F32), pltpu.VMEM((2, rank, rank), F32),
            pltpu.VMEM((2, rank, rank), F32), pltpu.VMEM((2, zs, rank // zs, rank), F32),
            pltpu.VMEM((2, rank, rank), F32), pltpu.VMEM((2, rank, rank), F32),
            dma((panels,)), dma, dma((panels,)), dma((panels, ys)), dma((panels, ys)),
            dma((ys, 2)), dma((ys,)), dma((panels, 2, ys)), dma((panels, ys)),
            dma((panels, number)), dma((panels, 2, 2, ysteps)), dma((panels, 2, 2, ysteps)),
            dma, dma, dma((2,)), dma((2,)), dma((listed, 2, zsteps)), dma((listed, 2, zsteps)),
            dma((2,)), dma((2,)), dma((2, zs)), dma((2, zs)), dma((2, zs)), dma((2, zs)),
            dma((2,)), dma((2,)), dma, dma((listed,)),
        ],
        compiler_params=pltpu.CompilerParams(
            collective_id=0, has_side_effects=True, vmem_limit_bytes=56 * 2 ** 20),
        name="updates",
    )(jnp.transpose(tile_list), left.reshape(panels, zs, CORES, own_rows, rank), right, probe)


def factors(rows, gram, scale):
    size, width = rows.shape
    rank = gram.shape[1]
    tiles = width // rank
    vmem = pl.BlockSpec(memory_space=pltpu.VMEM)
    hbm = pl.BlockSpec(memory_space=pl.ANY)
    return pl.pallas_call(
        functools.partial(factor_kernel, scale),
        out_shape=(jax.ShapeDtypeStruct((tiles, size, rank), F32),
                   jax.ShapeDtypeStruct((tiles, rank, rank), F32)),
        in_specs=[hbm, hbm],
        out_specs=(vmem, vmem),
        scratch_shapes=[pltpu.VMEM((size, width), F32), pltpu.VMEM((tiles * rank, rank), F32),
                        pltpu.SemaphoreType.DMA((2,))],
        compiler_params=pltpu.CompilerParams(vmem_limit_bytes=60 * 2 ** 20),
        name="factors",
    )(rows, gram)


def solution(mesh):
    rows, depth = mesh.shape["rows"], mesh.shape["depth"]

    def on_device(left_factors, right_factors, probe_matrix, tile_list):
        left, right = left_factors[0], right_factors[0]
        scale = math.sqrt(float(left.shape[1]))
        own_rows, gram = updates(tile_list, left, right, probe_matrix,
                                 XS, rows // XS, depth // CORES)
        gram = gram.reshape(-1, gram.shape[2])
        basis, lower = factors(own_rows, gram, scale)
        return basis[None], lower[None]

    in_specs = (P("rows", "depth", None, None), P("rows", "depth", None, None), P(), P())
    out_specs = (P("rows", None, "depth", None), P("rows", None, None, None))
    return jax.shard_map(
        on_device, mesh=mesh, in_specs=in_specs, out_specs=out_specs, check_vma=False
    )
```
